128 devices in a mesh: exp: 64 (over x, y, z), tp: 2 (over core).
Axes of the slice: x: 4, y: 4, z: 4, core: 2. Of those that a mesh axis runs over, the one named last changes fastest.
Arguments:
- tokens: bfloat16 [16384, 4096], P(('exp', 'tp')), may hold values from -6 to 6
- gate_weight: bfloat16 [64, 4096, 768], P('exp', None, 'tp'), may hold values from -0.09375 to 0.09375
- up_weight: bfloat16 [64, 4096, 768], P('exp', None, 'tp'), may hold values from -0.09375 to 0.09375
- down_weight: bfloat16 [64, 768, 4096], P('exp', 'tp'), may hold values from -0.21875 to 0.21875
- routes: int32 [16384, 8], P(('exp', 'tp')), may hold values from 0 to 63, all different within a row; in each aligned block of 128 rows (0 to 127, 128 to 255, ...) at most 18 rows name the same one
- gate_probs: float32 [16384, 8], P(('exp', 'tp')), may hold values from 0.02 to 0.5
- valid_mask: int32 [16384, 8], P(('exp', 'tp')), may hold values 0 or 1
Outputs:
- mixed: bfloat16 [16384, 4096], P(('exp', 'tp'))
- score_gate: bfloat16 [64, 4096, 768], P('exp', None, 'tp')
- score_up: bfloat16 [64, 4096, 768], P('exp', None, 'tp')
- score_down: bfloat16 [64, 768, 4096], P('exp', 'tp')
The draws below stay inside these ranges and needn't reach their ends.
Inputs may be any that keep to these rules, and one draw needn't show every extreme that they name: Among the rows of one device, no expert is named by more than 18 entries of routes, a bound that some block reaches; a row names 8 different experts.
All inputs are finite; a program needn't handle non-finite values. No bound on the sum of `valid_mask` on one device may be relied on, other than what follows from the above.
Results may differ from the reference program's by a relative error of at most 0.0065.
Values may be sent and summed in bfloat16 or wider, within the bound.
No kernel may reach another device: no remote copies, remote signals or barrier semaphores. Data moves between devices by JAX's collectives and lax.ppermute only.
A program may use at most 192 MiB of HBM per device.

```python
import math
import jax
import jax.numpy as jnp
import numpy as np
from jax import lax

D = 4096
FF_WIN = 768
TOP = 8
TOK_DEV = 128
EXPERTS = 64
TOKENS = 16384
CAP = 18
N_EXP = 64
N_TP = 2


def plant(drawn, stream_key, least, high):
    longest = drawn.shape.index(max(drawn.shape))
    spots = []
    for shift in (0, 1):
        where = [jax.random.randint(jax.random.fold_in(stream_key, axis), (), 0, length) for axis, length in enumerate(drawn.shape)]
        where[longest] = (where[longest] + shift) % drawn.shape[longest]
        spots.append(tuple(where))
    return drawn.at[spots[0]].set(least).at[spots[1]].set(high)


def steps_of(rng, shape, split, smallest, high):
    level, own = 1.0, jax.random.fold_in(rng, 6)
    for axis_at, blocks in split:
        draws = jnp.exp(jax.random.uniform(jax.random.fold_in(own, axis_at), (blocks,), jnp.float32, smallest / len(split), high / len(split)))
        level = level * jnp.repeat(draws, shape[axis_at] // blocks).reshape([-1 if axis == axis_at else 1 for axis in range(len(shape))])
    return level


def routed_block(stream_key, own, number, rows, amount, top, most, skew):
    sequence = jax.random.permutation(stream_key, amount)
    crowded, usual = portions_of(amount, rows * top, most, skew, True), portions_of(amount, rows * top, most, skew, False)
    places = jnp.arange(amount)

    def named(sizes, turn):
        used = int((sizes > 0).sum())
        fixed = max(1, used // 4)
        moved = fixed + (places - fixed + turn * (used - fixed)) % max(1, amount - fixed)
        return jnp.zeros((amount,), jnp.int32).at[sequence[jnp.where(places < fixed, places, moved)]].set(jnp.asarray(sizes, jnp.int32))

    sizes = jnp.where(number % 4 == 0, named(crowded, number // 4), named(usual, number - number // 4 - 1))
    mixed = jax.random.permutation(jax.random.fold_in(own, 3), amount)
    source_of, sink = mixed[0:amount // 2 * 2:2], mixed[1:amount // 2 * 2:2]
    margin = jnp.minimum(sizes[source_of] - 1, most - sizes[sink]) // 2
    margin = jnp.where((source_of == sequence[0]) | (sink == sequence[0]) | (sizes[sink] == 0), 0, jnp.maximum(margin, 0))
    moved = jax.random.randint(jax.random.fold_in(own, 4), (amount // 2,), 0, 1 << 20) % (margin + 1)
    sizes = sizes.at[source_of].add(-moved).at[sink].add(moved)
    labels = jnp.searchsorted(jnp.cumsum(sizes), jnp.arange(rows * top), side="right").astype(jnp.int32)
    grid = labels.reshape(top, rows).T
    grid = grid[jax.random.permutation(jax.random.fold_in(own, 1), rows)]
    turn = jax.random.randint(jax.random.fold_in(own, 2), (rows, 1), 0, top)
    return jnp.take_along_axis(grid, (jnp.arange(top)[None, :] + turn) % top, axis=1)


def portions_of(count, total, reach, slope, full):
    loads = [(1 << 20) // math.isqrt(rank ** slope) + 1 for rank in range(1, count + 1)]
    largest = reach if full else min(reach, max(-(-total // count), total * loads[0] // sum(loads)))
    least = 1 if total - largest >= count - 1 else 0
    given, rest = [largest] + [least] * (count - 1), total - largest - least * (count - 1)
    while rest > 0:
        candidates = [i for i in range(1, count) if given[i] < largest] or [i for i in range(1, count) if given[i] < reach]
        pool, budget = sum([loads[i] for i in candidates]), rest
        for i in candidates:
            more = min(reach - given[i], max(1, budget * loads[i] // pool), rest)
            given[i] = given[i] + more
            rest = rest - more
    return np.array(given)


def centred(rng, extent, deviation, limit, cuts=(), kind=jnp.bfloat16):
    factor_of = steps_of(rng, extent, cuts, -0.22, 0.18) if cuts else 1.0
    array = jax.random.normal(rng, extent, jnp.float32) * deviation * factor_of
    return jnp.minimum(jnp.maximum(array, -limit), limit).astype(kind)


def setup_inputs(seed: int = 0) -> dict:
    seeds = jax.random.split(jax.random.key(seed), 8)
    tokens = centred(seeds[0], (TOKENS, D), 1.0, 6.0, ((0, 128),))
    gate_weight = centred(seeds[1], (EXPERTS, D, FF_WIN), D ** -0.5, 0.09375, ((0, 64), (2, 2)))
    up_weight = centred(seeds[2], (EXPERTS, D, FF_WIN), D ** -0.5, 0.09375, ((0, 64), (2, 2)))
    down_weight = centred(seeds[3], (EXPERTS, FF_WIN, D), FF_WIN ** -0.5, 0.21875, ((0, 64), (1, 2)))
    routes_keys = jax.random.split(jax.random.fold_in(seeds[4], 1), TOKENS // TOK_DEV)
    routes_turns = jax.random.permutation(jax.random.fold_in(seeds[4], 3), TOKENS // TOK_DEV)
    routes = jax.vmap(lambda own, number: routed_block(jax.random.fold_in(seeds[4], 2), own, number, TOK_DEV, EXPERTS, TOP, CAP, 2))(routes_keys, routes_turns).reshape((TOKENS, TOP))
    gate_probs = jnp.clip(jnp.exp(math.log(0.5) - 3.218876 * jax.random.uniform(seeds[5], (TOKENS, TOP), jnp.float32) ** steps_of(seeds[5], (TOKENS, TOP), ((0, 128),), -0.2, 0.2)), 0.02, 0.5)
    valid_mask = plant((jax.random.randint(seeds[6], (TOKENS, TOP), 0, 8) < 7).astype(jnp.int32), jax.random.fold_in(seeds[6], 1), 0, 1)
    return {"tokens": tokens, "gate_weight": gate_weight, "up_weight": up_weight, "down_weight": down_weight, "routes": routes, "gate_probs": gate_probs, "valid_mask": valid_mask}


def reference(tokens, gate_weight, up_weight, down_weight, routes, gate_probs, valid_mask):
    flat_routes = routes.reshape(-1).astype(jnp.int32)
    live_flat = valid_mask.reshape(-1) > 0
    combine_w = jnp.where(live_flat, gate_probs.reshape(-1), 0.0).astype(jnp.float32)
    sent_w = lax.optimization_barrier(combine_w.astype(jnp.bfloat16)).astype(jnp.float32)
    most_rows = CAP * N_EXP * N_TP
    slice_width = FF_WIN // N_TP

    def per_expert(running, inputs):
        expert_id, w_gate, w_up, w_down = inputs
        chosen = live_flat & (flat_routes == expert_id)
        chosen_pos = jnp.nonzero(chosen, size=most_rows, fill_value=0)[0]
        chosen_count = jnp.sum(chosen.astype(jnp.int32))
        still_live = jnp.arange(most_rows, dtype=jnp.int32) < chosen_count
        row_weight = jnp.where(still_live, sent_w[chosen_pos], 0.0)
        mix_weight = jnp.where(still_live, combine_w[chosen_pos], 0.0)
        token_ids = chosen_pos // TOP
        picked = tokens[token_ids]
        gate_proj = jnp.dot(picked, w_gate, preferred_element_type=jnp.float32)
        up_proj = jnp.dot(picked, w_up, preferred_element_type=jnp.float32)
        hidden = (jax.nn.silu(gate_proj) * up_proj).astype(jnp.bfloat16)
        input_sq = jnp.dot(row_weight, jnp.square(picked.astype(jnp.float32)), precision=lax.Precision.HIGHEST)
        hidden_sq = jnp.dot(row_weight, jnp.square(hidden.astype(jnp.float32)), precision=lax.Precision.HIGHEST)
        expert_out = jnp.zeros((most_rows, D), jnp.float32)
        for half_id in range(N_TP):
            lower_edge = half_id * slice_width
            partial_out = jnp.dot(hidden[:, lower_edge:lower_edge + slice_width], w_down[lower_edge:lower_edge + slice_width], preferred_element_type=jnp.float32)
            expert_out = expert_out + lax.optimization_barrier(partial_out.astype(jnp.bfloat16)).astype(jnp.float32)
        expert_out = expert_out.astype(jnp.bfloat16)
        running = running.at[token_ids].add(mix_weight[:, None] * expert_out.astype(jnp.float32))
        input_norm = jnp.sqrt(input_sq)
        score_gate = (jnp.abs(w_gate.astype(jnp.float32)) * input_norm[:, None]).astype(jnp.bfloat16)
        score_up = (jnp.abs(w_up.astype(jnp.float32)) * input_norm[:, None]).astype(jnp.bfloat16)
        score_down = (jnp.abs(w_down.astype(jnp.float32)) * jnp.sqrt(hidden_sq)[:, None]).astype(jnp.bfloat16)
        return (running, (score_gate, score_up, score_down))
    mixed_sum, scores = lax.scan(per_expert, jnp.zeros((TOKENS, D), jnp.float32), (jnp.arange(EXPERTS, dtype=jnp.int32), gate_weight, up_weight, down_weight))
    return (mixed_sum.astype(jnp.bfloat16), scores[0], scores[1], scores[2])
```

```python
import functools

import jax
import jax.numpy as jnp
from jax import lax
from jax.experimental import pallas as pl
from jax.experimental.pallas import tpu as pltpu
from jax.sharding import PartitionSpec as P

BF16, F32 = jnp.bfloat16, jnp.float32
CHUNK = 512
VMEM = 56 * 1024 * 1024


def iota(shape, dim):
    return lax.broadcasted_iota(jnp.int32, shape, dim)


def flip_rows(values):
    count = values.shape[0]
    eye = (iota((count, count), 0) == iota((count, count), 1)).astype(BF16)
    return lax.dot_general(values.astype(BF16), eye, (((0,), (0,)), ((), ())), preferred_element_type=F32)


def pick_chunk(chunk, base, blocks, extra, slots):
    shape = (blocks * extra, blocks * slots)
    row, col = iota(shape, 0), iota(shape, 1)
    return (col == (row // extra) * slots + chunk * extra + row % extra + base).astype(BF16)


def build_kernel(experts, slots, extra, chunks, routes, valid, probs, tok, out, slot_scr, sel_scr, acc_scr, w_scr):
    i = pl.program_id(0)
    count = routes.shape[0]
    rows = experts * slots

    def grouped(make):
        return make(slot_scr[...].reshape(experts, 1, count), iota((experts, slots, count), 1))

    @pl.when(i == 0)
    def _():
        r_t, v_t, p_t = (flip_rows(ref[...].astype(F32)) for ref in (routes, valid, probs))
        ids = iota((experts, count), 0).astype(F32)
        named, weight = jnp.zeros((experts, count), F32), jnp.zeros((experts, count), F32)
        for k in range(routes.shape[1]):
            hit = (r_t[k : k + 1, :] == ids) & (v_t[k : k + 1, :] > 0)
            named = named + jnp.where(hit, 1.0, 0.0)
            weight = weight + jnp.where(hit, p_t[k : k + 1, :], 0.0)
        before = (iota((count, count), 0) < iota((count, count), 1)).astype(BF16)
        place = jnp.dot(named.astype(BF16), before, preferred_element_type=F32)
        slot_scr[...] = jnp.where(named > 0, place, -1.0)
        hits = grouped(lambda slot, row: jnp.where(slot == row.astype(F32), 1.0, 0.0))
        sel_scr[...] = hits.reshape(rows, count).astype(BF16)
        more = grouped(
            lambda slot, row: jnp.where((slot == (row + slots).astype(F32)) & (row < extra), 1.0, 0.0)
        )
        weight = weight.reshape(experts, 1, count)
        w_main = jnp.sum(hits * weight, axis=2, keepdims=True)
        w_more = jnp.sum(more * weight, axis=2, keepdims=True)
        lane = iota((experts, slots, 128), 2)
        packed = jnp.where(lane == 0, w_main, jnp.where(lane == 1, w_more, 0.0))
        w_scr[...] = packed.reshape(rows, 128).astype(BF16)
        acc_scr[...] = jnp.zeros_like(acc_scr)

    @pl.when(i < chunks)
    def _():
        out[...] = jnp.dot(sel_scr[...], tok[...], preferred_element_type=F32).astype(BF16)
        more = grouped(
            lambda slot, row: jnp.where(
                (slot == (row % extra + slots).astype(F32)) & (row // extra == i), 1.0, 0.0
            )
        )
        acc_scr[...] += jnp.dot(
            more.reshape(rows, count).astype(BF16), tok[...], preferred_element_type=F32
        )

    @pl.when(i == chunks)
    def _():
        out[...] = acc_scr[...].astype(BF16)

    @pl.when(i == chunks + 1)
    def _():
        out[:, 0:128] = w_scr[...]


def build(routes, valid, probs, tokens, experts, slots, extra):
    count, width = tokens.shape
    chunks = width // CHUNK
    rows = experts * slots
    small = pl.BlockSpec((count, routes.shape[1]), lambda i: (0, 0))
    return pl.pallas_call(
        functools.partial(build_kernel, experts, slots, extra, chunks),
        grid=(chunks + 2,),
        in_specs=[small, small, small, pl.BlockSpec((count, CHUNK), lambda i: (0, jnp.minimum(i, chunks - 1)))],
        out_specs=pl.BlockSpec((rows, CHUNK), lambda i: (0, i)),
        out_shape=jax.ShapeDtypeStruct((rows, width + CHUNK + 128), BF16),
        scratch_shapes=[
            pltpu.VMEM((experts, count), F32),
            pltpu.VMEM((rows, count), BF16),
            pltpu.VMEM((rows, CHUNK), F32),
            pltpu.VMEM((rows, 128), BF16),
        ],
        compiler_params=pltpu.CompilerParams(vmem_limit_bytes=VMEM),
        cost_estimate=pl.CostEstimate(flops=4 * rows * count * width, bytes_accessed=2 * rows * width, transcendentals=0),
    )(routes, valid, probs, tokens)


def expert_kernel(blocks, slots, extra, chunks, x, x_more, x_w, wg0, wg1, wu0, wu1, wd0, wd1, out, sq_in, sq_hid,
                  xs, acc0, acc1, hid, w_col, acc_more):
    i = pl.program_id(0)
    rows, more = blocks * slots, blocks * extra
    half = wg0.shape[1]

    @pl.when(i == 0)
    def _():
        acc0[...] = jnp.zeros_like(acc0)
        acc1[...] = jnp.zeros_like(acc1)
        acc_more[...] = jnp.zeros_like(acc_more)
        w_main = x_w[...].astype(F32)
        w_more = jnp.dot(pick_chunk(0, 0, blocks, extra, slots), x_w[...], preferred_element_type=F32)
        w_col[0:rows, :] = jnp.broadcast_to(w_main[:, 0:1], (rows, 128))
        w_col[rows : rows + more, :] = jnp.broadcast_to(w_more[:, 1:2], (more, 128))

    @pl.when(i < chunks)
    def _():
        xs[0:rows, :] = x[...]
        xs[rows : rows + more, :] = jnp.dot(
            pick_chunk(i, 0, blocks, extra, slots), x_more[...], preferred_element_type=F32
        ).astype(BF16)
        acc0[...] += jnp.dot(xs[...], jnp.concatenate([wg0[...], wu0[...]], axis=1), preferred_element_type=F32)
        acc1[...] += jnp.dot(xs[...], jnp.concatenate([wg1[...], wu1[...]], axis=1), preferred_element_type=F32)
        for lane in range(0, CHUNK, 128):
            part = xs[:, lane : lane + 128].astype(F32)
            sq_in[:, lane : lane + 128] = jnp.sum(part * part * w_col[...], axis=0, keepdims=True)

    @pl.when(i == chunks)
    def _():
        for at, acc in ((0, acc0), (half, acc1)):
            for lane in range(0, half, 128):
                gate = acc[:, lane : lane + 128]
                up = acc[:, half + lane : half + lane + 128]
                value = (gate / (1.0 + jnp.exp(-gate)) * up).astype(BF16)
                hid[:, at + lane : at + lane + 128] = value
                value = value.astype(F32)
                sq_hid[:, at + lane : at + lane + 128] = jnp.sum(value * value * w_col[...], axis=0, keepdims=True)

    @pl.when((i >= chunks) & (i < 2 * chunks))
    def _():
        result = jnp.dot(
            hid[...], jnp.concatenate([wd0[...], wd1[...]], axis=0), preferred_element_type=F32
        ).astype(BF16)
        out[...] = result[0:rows]
        shape = (rows, more)
        row, col = iota(shape, 0), iota(shape, 1)
        spread = (row == (col // extra) * slots + (i - chunks) * extra + col % extra).astype(BF16)
        acc_more[...] += jnp.dot(spread, result[rows : rows + more], preferred_element_type=F32)

    @pl.when(i == 2 * chunks)
    def _():
        out[...] = acc_more[...].astype(BF16)


def expert(received, wg0, wg1, wu0, wu1, wd0, wd1, blocks, slots, extra):
    width, half = wg0.shape
    chunks = width // CHUNK
    rows, more = blocks * slots, blocks * extra
    up_to = lambda i: jnp.minimum(i, chunks - 1)
    after = lambda i: jnp.clip(i - chunks, 0, chunks - 1)
    w_in = pl.BlockSpec((CHUNK, half), lambda i: (up_to(i), 0))
    w_out = pl.BlockSpec((half, CHUNK), lambda i: (0, after(i)))
    return pl.pallas_call(
        functools.partial(expert_kernel, blocks, slots, extra, chunks),
        grid=(2 * chunks + 1,),
        in_specs=[
            pl.BlockSpec((rows, CHUNK), lambda i: (0, up_to(i))),
            pl.BlockSpec((rows, CHUNK), lambda i: (0, chunks)),
            pl.BlockSpec((rows, 128), lambda i: (0, (width + CHUNK) // 128)),
            w_in, w_in, w_in, w_in, w_out, w_out,
        ],
        out_specs=[
            pl.BlockSpec((rows, CHUNK), lambda i: (0, jnp.maximum(i - chunks, 0))),
            pl.BlockSpec((1, CHUNK), lambda i: (0, up_to(i))),
            pl.BlockSpec((1, 2 * half), lambda i: (0, 0)),
        ],
        out_shape=[
            jax.ShapeDtypeStruct((rows, width + CHUNK), BF16),
            jax.ShapeDtypeStruct((1, width), F32),
            jax.ShapeDtypeStruct((1, 2 * half), F32),
        ],
        scratch_shapes=[
            pltpu.VMEM((rows + more, CHUNK), BF16),
            pltpu.VMEM((rows + more, 2 * half), F32),
            pltpu.VMEM((rows + more, 2 * half), F32),
            pltpu.VMEM((rows + more, 2 * half), BF16),
            pltpu.VMEM((rows + more, 128), F32),
            pltpu.VMEM((rows, CHUNK), F32),
        ],
        compiler_params=pltpu.CompilerParams(vmem_limit_bytes=VMEM),
        cost_estimate=pl.CostEstimate(
            flops=12 * (rows + more) * width * half, bytes_accessed=4 * rows * width + 12 * width * half, transcendentals=0
        ),
    )(received, received, received, wg0, wg1, wu0, wu1, wd0, wd1)


def combine_kernel(experts, slots, extra, chunks, routes, valid, probs, x, x_more, out, slot_scr, w_scr, sel_scr):
    i = pl.program_id(0)
    count = routes.shape[0]
    rows = experts * slots
    row_of = iota((count, rows), 1) % slots

    @pl.when(i == 0)
    def _():
        ids = iota((count, experts), 1)
        named, weight = jnp.zeros((count, experts), F32), jnp.zeros((count, experts), F32)
        for k in range(routes.shape[1]):
            hit = (routes[:, k : k + 1] == ids) & (valid[:, k : k + 1] > 0)
            named = named + jnp.where(hit, 1.0, 0.0)
            weight = weight + jnp.where(hit, probs[:, k : k + 1], 0.0)
        before = (iota((count, count), 1) < iota((count, count), 0)).astype(BF16)
        place = jnp.dot(before, named.astype(BF16), preferred_element_type=F32)
        slot = jnp.where(named > 0, place, -1.0).astype(BF16)
        widen = (iota((experts, rows), 1) // slots == iota((experts, rows), 0)).astype(BF16)
        slot_scr[...] = jnp.dot(slot, widen, preferred_element_type=F32)
        w_scr[...] = jnp.dot(weight.astype(BF16), widen, preferred_element_type=F32)
        sel_scr[...] = jnp.where(slot_scr[...] == row_of.astype(F32), w_scr[...], 0.0).astype(BF16)

    more = (slot_scr[...] == (row_of % extra + slots).astype(F32)) & (row_of // extra == i)
    total = jnp.dot(sel_scr[...], x[...], preferred_element_type=F32)
    total += jnp.dot(jnp.where(more, w_scr[...], 0.0).astype(BF16), x_more[...], preferred_element_type=F32)
    out[...] = total.astype(BF16)


def combine(routes, valid, probs, returned, experts, slots, extra):
    rows, wide = returned.shape
    width = wide - CHUNK
    chunks = width // CHUNK
    count = routes.shape[0]
    small = pl.BlockSpec((count, routes.shape[1]), lambda i: (0, 0))
    return pl.pallas_call(
        functools.partial(combine_kernel, experts, slots, extra, chunks),
        grid=(chunks,),
        in_specs=[small, small, small, pl.BlockSpec((rows, CHUNK), lambda i: (0, i)),
                  pl.BlockSpec((rows, CHUNK), lambda i: (0, chunks))],
        out_specs=pl.BlockSpec((count, CHUNK), lambda i: (0, i)),
        out_shape=jax.ShapeDtypeStruct((count, width), BF16),
        scratch_shapes=[
            pltpu.VMEM((count, rows), F32),
            pltpu.VMEM((count, rows), F32),
            pltpu.VMEM((count, rows), BF16),
        ],
        compiler_params=pltpu.CompilerParams(vmem_limit_bytes=VMEM),
        cost_estimate=pl.CostEstimate(flops=4 * rows * count * width, bytes_accessed=2 * rows * wide, transcendentals=0),
    )(routes, valid, probs, returned, returned)


def swap(value):
    return lax.ppermute(value, "tp", [(0, 1), (1, 0)])


def exchange(value, experts, slots):
    value = value.reshape(experts, slots, value.shape[1])
    value = lax.all_to_all(value, "exp", split_axis=0, concat_axis=0, tiled=True)
    return value.reshape(experts * slots, value.shape[2])


def per_device(tokens, gate_weight, up_weight, down_weight, routes, gate_probs, valid_mask):
    count, top = routes.shape
    experts = lax.axis_size("exp")
    cap = max(2, count * top * 9 // (8 * experts))
    extra = 2
    slots = cap - extra
    w_gate, w_up, w_down = gate_weight[0], up_weight[0], down_weight[0]
    half = w_gate.shape[1]
    o_gate, o_up, o_down = swap(w_gate), swap(w_up), swap(w_down)
    sent = build(routes, valid_mask, gate_probs, tokens, experts, slots, extra)
    received = exchange(sent, experts, slots)
    outs, sq_in, sq_hid = expert(
        received, w_gate, o_gate, w_up, o_up, w_down, o_down, experts, slots, extra
    )
    returned = exchange(outs, experts, slots)
    mixed = combine(routes, valid_mask, gate_probs, returned, experts, slots, extra)
    other = swap(jnp.concatenate([sq_in[0], sq_hid[0, half:]]))
    both = jnp.sqrt(jnp.concatenate([sq_in[0], sq_hid[0, :half]]) + other)
    in_norm, hid_norm = both[: tokens.shape[1], None], both[tokens.shape[1] :, None]
    score_gate = (jnp.abs(w_gate.astype(F32)) * in_norm).astype(BF16)
    score_up = (jnp.abs(w_up.astype(F32)) * in_norm).astype(BF16)
    score_down = (jnp.abs(w_down.astype(F32)) * hid_norm).astype(BF16)
    return (mixed, score_gate[None], score_up[None], score_down[None])


def solution(mesh):
    in_specs = (
        P(("exp", "tp"), None),
        P("exp", None, "tp"),
        P("exp", None, "tp"),
        P("exp", "tp", None),
        P(("exp", "tp"), None),
        P(("exp", "tp"), None),
        P(("exp", "tp"), None),
    )
    out_specs = (
        P(("exp", "tp"), None),
        P("exp", None, "tp"),
        P("exp", None, "tp"),
        P("exp", "tp", None),
    )
    return jax.shard_map(
        per_device, mesh=mesh, in_specs=in_specs, out_specs=out_specs, check_vma=False
    )
```

```python
import functools

import jax
import jax.numpy as jnp
from jax import lax
from jax.experimental import pallas as pl
from jax.experimental.pallas import tpu as pltpu
from jax.sharding import PartitionSpec as P

BF16, F32 = jnp.bfloat16, jnp.float32
CHUNK = 512
WIDE = 1024
VMEM = 56 * 1024 * 1024


def iota(shape, dim):
    return lax.broadcasted_iota(jnp.int32, shape, dim)


def one_hot(match):
    return jnp.where(match, 1.0, 0.0).astype(BF16)


def by_chunk(blocks, extra, slots):
    more, shape = blocks * extra, (slots // extra * blocks * extra, blocks * slots)
    row = iota((shape[0], 1), 0)
    home = (row % more) // extra * slots + row // more * extra + row % extra
    return one_hot(home == iota(shape, 1))


def by_block(blocks, extra, slots):
    more, shape = blocks * extra, (blocks * slots, slots // extra * blocks * extra)
    row = iota((shape[0], 1), 0)
    home = row % slots // extra * more + row // slots * extra + row % extra
    return one_hot(home == iota(shape, 1))


def assign(experts, routes, valid, probs):
    count = routes.shape[1]
    ids = iota((experts, count), 0)
    named, weight = jnp.zeros((experts, count), F32), jnp.zeros((experts, count), F32)
    for k in range(routes.shape[0]):
        hit = (routes[k : k + 1, :] == ids) & (valid[k : k + 1, :] > 0)
        named = named + jnp.where(hit, 1.0, 0.0)
        weight = weight + jnp.where(hit, probs[k : k + 1, :], 0.0)
    before = one_hot(iota((count, count), 0) < iota((count, count), 1))
    place = jnp.dot(named.astype(BF16), before, preferred_element_type=F32)
    return jnp.where(named > 0, place, -1.0).astype(jnp.int32), weight


def build_kernel(experts, slots, extra, chunks, routes, valid, probs, tok, out, slot_scr, sel_scr, stack, w_scr):
    i = pl.program_id(0)
    count = routes.shape[1]
    rows = experts * slots
    row = iota((experts, slots, count), 1)

    @pl.when(i == 0)
    def _():
        slot, weight = assign(experts, routes, valid, probs)
        slot_scr[...] = slot
        slot, weight = slot.reshape(experts, 1, count), weight.reshape(experts, 1, count)
        hits = slot == row
        sel_scr[...] = jnp.where(hits, 1.0, 0.0).reshape(rows, count).astype(BF16)
        w_main = jnp.sum(jnp.where(hits, weight, 0.0), axis=2, keepdims=True)
        w_more = jnp.sum(jnp.where((slot == row + slots) & (row < extra), weight, 0.0), axis=2, keepdims=True)
        lane = iota((experts, slots, 128), 2)
        packed = jnp.where(lane == 0, w_main, jnp.where(lane == 1, w_more, 0.0))
        w_scr[...] = packed.reshape(rows, 128).astype(BF16)

    @pl.when(i < chunks)
    def _():
        out[...] = jnp.dot(sel_scr[...], tok[...], preferred_element_type=F32).astype(BF16)
        for part in range(WIDE // CHUNK):
            at = pl.multiple_of((i * (WIDE // CHUNK) + part) * count, count)
            stack[pl.ds(at, count), :] = tok[:, part * CHUNK : (part + 1) * CHUNK]

    @pl.when(i == chunks)
    def _():
        slot = slot_scr[...].reshape(experts, 1, count)
        wanted = jnp.where(slot == row % extra + slots, row // extra, -1).reshape(rows, count)
        pick = jnp.concatenate([one_hot(wanted == c) for c in range(slots // extra)], axis=1)
        total = jnp.dot(pick, stack[...], preferred_element_type=F32)
        out[:, 0:CHUNK] = total.astype(BF16)
        out[:, CHUNK : CHUNK + 128] = w_scr[...]


def build(routes, valid, probs, tokens, experts, slots, extra):
    count, width = tokens.shape
    chunks = width // WIDE
    rows = experts * slots
    small = pl.BlockSpec((routes.shape[0], count), lambda i: (0, 0))
    return pl.pallas_call(
        functools.partial(build_kernel, experts, slots, extra, chunks),
        grid=(chunks + 1,),
        in_specs=[small, small, small, pl.BlockSpec((count, WIDE), lambda i: (0, jnp.minimum(i, chunks - 1)))],
        out_specs=pl.BlockSpec((rows, WIDE), lambda i: (0, i)),
        out_shape=jax.ShapeDtypeStruct((rows, width + CHUNK + 128), BF16),
        scratch_shapes=[
            pltpu.VMEM((experts, count), jnp.int32),
            pltpu.VMEM((rows, count), BF16),
            pltpu.VMEM((width // CHUNK * count, CHUNK), BF16),
            pltpu.VMEM((rows, 128), BF16),
        ],
        compiler_params=pltpu.CompilerParams(vmem_limit_bytes=VMEM),
        cost_estimate=pl.CostEstimate(flops=4 * rows * count * width, bytes_accessed=2 * rows * width, transcendentals=0),
    )(routes, valid, probs, tokens)


def unpack_kernel(blocks, slots, extra, x_more, x_w, wd, more, w_col, wd_copy):
    rows, count = blocks * slots, blocks * extra
    wd_copy[...] = wd[...]

    @pl.when(pl.program_id(0) == 0)
    def _():
        pick = by_chunk(blocks, extra, slots)
        more[...] = jnp.dot(pick, x_more[...], preferred_element_type=F32).astype(BF16)
        w_main = x_w[...].astype(F32)
        w_more = jnp.dot(pick[0:count], x_w[...], preferred_element_type=F32)
        w_col[0:rows, :] = jnp.broadcast_to(w_main[:, 0:1], (rows, 128))
        w_col[rows : rows + count, :] = jnp.broadcast_to(w_more[:, 1:2], (count, 128))


def unpack(received, wd, blocks, slots, extra):
    half, width = wd.shape
    rows, count = blocks * slots, blocks * extra
    flat = pl.BlockSpec((half, WIDE), lambda i: (0, i))
    return pl.pallas_call(
        functools.partial(unpack_kernel, blocks, slots, extra),
        grid=(width // WIDE,),
        in_specs=[
            pl.BlockSpec((rows, CHUNK), lambda i: (0, width // CHUNK)),
            pl.BlockSpec((rows, 128), lambda i: (0, (width + CHUNK) // 128)),
            flat,
        ],
        out_specs=[
            pl.BlockSpec((rows, CHUNK), lambda i: (0, 0)),
            pl.BlockSpec((rows + count, 128), lambda i: (0, 0)),
            flat,
        ],
        out_shape=[
            jax.ShapeDtypeStruct((rows, CHUNK), BF16),
            jax.ShapeDtypeStruct((rows + count, 128), F32),
            jax.ShapeDtypeStruct(wd.shape, BF16),
        ],
        compiler_params=pltpu.CompilerParams(vmem_limit_bytes=VMEM),
        cost_estimate=pl.CostEstimate(flops=2 * rows * rows * CHUNK, bytes_accessed=4 * rows * CHUNK, transcendentals=0),
    )(received, received, wd)


def hidden_kernel(blocks, slots, extra, chunks, x, x_more, w_col, wg0, wg1, wu0, wu1, hid, sq, xs, acc0, acc1):
    i = pl.program_id(0)
    rows, more = blocks * slots, blocks * extra
    half = wg0.shape[1]
    parts = WIDE // CHUNK

    @pl.when(i == 0)
    def _():
        acc0[...] = jnp.zeros_like(acc0)
        acc1[...] = jnp.zeros_like(acc1)

    @pl.when(i < chunks)
    def _():
        xs[0:rows, :] = x[...]
        for part in range(parts):
            at = pl.multiple_of((i * parts + part) * more, more)
            xs[rows : rows + more, part * CHUNK : (part + 1) * CHUNK] = x_more[pl.ds(at, more), :]
        acc0[...] += jnp.dot(xs[...], jnp.concatenate([wg0[...], wu0[...]], axis=1), preferred_element_type=F32)
        acc1[...] += jnp.dot(xs[...], jnp.concatenate([wg1[...], wu1[...]], axis=1), preferred_element_type=F32)
        for lane in range(0, WIDE, 128):
            part = xs[:, lane : lane + 128].astype(F32)
            sq[:, lane : lane + 128] = jnp.sum(part * part * w_col[...], axis=0, keepdims=True)

    @pl.when(i == chunks)
    def _():
        sq[...] = jnp.zeros_like(sq)
        for at, acc in ((0, acc0), (half, acc1)):
            for lane in range(0, half, 128):
                gate = acc[:, lane : lane + 128]
                up = acc[:, half + lane : half + lane + 128]
                value = (gate / (1.0 + jnp.exp(-gate)) * up).astype(BF16)
                hid[:, at + lane : at + lane + 128] = value
                value = value.astype(F32)
                sq[:, at + lane : at + lane + 128] = jnp.sum(value * value * w_col[...], axis=0, keepdims=True)


def hidden_units(received, x_more, w_col, wg0, wg1, wu0, wu1, blocks, slots, extra):
    width, half = wg0.shape
    chunks = width // WIDE
    rows, more = blocks * slots, blocks * extra
    up_to = lambda i: jnp.minimum(i, chunks - 1)
    w_in = pl.BlockSpec((WIDE, half), lambda i: (up_to(i), 0))
    return pl.pallas_call(
        functools.partial(hidden_kernel, blocks, slots, extra, chunks),
        grid=(chunks + 1,),
        in_specs=[
            pl.BlockSpec((rows, WIDE), lambda i: (0, up_to(i))),
            pl.BlockSpec((rows, CHUNK), lambda i: (0, 0)),
            pl.BlockSpec((rows + more, 128), lambda i: (0, 0)),
            w_in, w_in, w_in, w_in,
        ],
        out_specs=[
            pl.BlockSpec((rows + more, 2 * half), lambda i: (0, 0)),
            pl.BlockSpec((1, WIDE), lambda i: (0, i)),
        ],
        out_shape=[
            jax.ShapeDtypeStruct((rows + more, 2 * half), BF16),
            jax.ShapeDtypeStruct((1, width + WIDE), F32),
        ],
        scratch_shapes=[
            pltpu.VMEM((rows + more, WIDE), BF16),
            pltpu.VMEM((rows + more, 2 * half), F32),
            pltpu.VMEM((rows + more, 2 * half), F32),
        ],
        compiler_params=pltpu.CompilerParams(vmem_limit_bytes=VMEM),
        cost_estimate=pl.CostEstimate(
            flops=8 * (rows + more) * width * half, bytes_accessed=2 * rows * width + 8 * width * half, transcendentals=0
        ),
    )(received, x_more, w_col, wg0, wg1, wu0, wu1)


def down_kernel(blocks, slots, extra, chunks, hid, wd0, wd1, out, stack):
    i = pl.program_id(0)
    rows, more = blocks * slots, blocks * extra
    parts = WIDE // CHUNK

    @pl.when(i < chunks)
    def _():
        result = jnp.dot(
            hid[...], jnp.concatenate([wd0[...], wd1[...]], axis=0), preferred_element_type=F32
        ).astype(BF16)
        out[...] = result[0:rows]
        for part in range(parts):
            at = pl.multiple_of((i * parts + part) * more, more)
            stack[pl.ds(at, more), :] = result[rows : rows + more, part * CHUNK : (part + 1) * CHUNK]

    @pl.when(i == chunks)
    def _():
        out[:, 0:CHUNK] = jnp.dot(
            by_block(blocks, extra, slots), stack[...], preferred_element_type=F32
        ).astype(BF16)


def down(hid, wd0, wd1, blocks, slots, extra):
    half, width = wd0.shape
    chunks = width // WIDE
    rows = blocks * slots
    w_out = pl.BlockSpec((half, WIDE), lambda i: (0, jnp.minimum(i, chunks - 1)))
    return pl.pallas_call(
        functools.partial(down_kernel, blocks, slots, extra, chunks),
        grid=(chunks + 1,),
        in_specs=[pl.BlockSpec(hid.shape, lambda i: (0, 0)), w_out, w_out],
        out_specs=pl.BlockSpec((rows, WIDE), lambda i: (0, i)),
        out_shape=jax.ShapeDtypeStruct((rows, width + CHUNK), BF16),
        scratch_shapes=[pltpu.VMEM((rows, CHUNK), BF16)],
        compiler_params=pltpu.CompilerParams(vmem_limit_bytes=VMEM),
        cost_estimate=pl.CostEstimate(
            flops=4 * hid.shape[0] * width * half, bytes_accessed=2 * rows * width + 4 * width * half, transcendentals=0
        ),
    )(hid, wd0, wd1)


def after(value, *first):
    anywhere = pl.BlockSpec(memory_space=pl.ANY)
    return pl.pallas_call(
        lambda *refs: None,
        in_specs=[anywhere] * (1 + len(first)),
        out_specs=anywhere,
        out_shape=jax.ShapeDtypeStruct(value.shape, value.dtype),
        input_output_aliases={0: 0},
        cost_estimate=pl.CostEstimate(flops=0, bytes_accessed=0, transcendentals=0),
    )(value, *first)


def column(line):
    eye = iota((128, 128), 0) == iota((128, 128), 1)
    return jnp.concatenate(
        [
            jnp.sum(jnp.where(eye, line[:, at : at + 128], 0.0), axis=1, keepdims=True)
            for at in range(0, line.shape[1], 128)
        ],
        axis=0,
    )


def combine_kernel(experts, slots, extra, chunks, routes, valid, probs, x, x_more, own, other, own_hid, other_hid, wg, wu, wd,
                   out, s_gate, s_up, s_down, sel_scr, more_scr, stack):
    i = pl.program_id(0)
    count = routes.shape[1]
    rows, more = experts * slots, experts * extra

    @pl.when(i == 0)
    def _():
        slot, weight = assign(experts, routes, valid, probs)
        slot, weight = slot.reshape(experts, 1, count), weight.reshape(experts, 1, count)
        hits = slot == iota((experts, slots, count), 1)
        sel_scr[...] = jnp.where(hits, weight, 0.0).reshape(rows, count).T.astype(BF16)
        late = [jnp.where(slot == slots + r, weight, 0.0).reshape(experts, count) for r in range(extra)]
        widen = [one_hot(iota((more, experts), 0) == iota((more, experts), 1) * extra + r) for r in range(extra)]
        spread = sum(
            jnp.dot(w, l.astype(BF16), preferred_element_type=F32) for w, l in zip(widen, late)
        )
        more_scr[...] = spread.T.astype(BF16)
        stack[...] = jnp.dot(
            by_chunk(experts, extra, slots), x_more[...], preferred_element_type=F32
        ).astype(BF16)

    total = jnp.dot(sel_scr[...], x[...], preferred_element_type=F32)
    for part in range(WIDE // CHUNK):
        at = pl.multiple_of((i * (WIDE // CHUNK) + part) * more, more)
        lanes = slice(part * CHUNK, (part + 1) * CHUNK)
        out[:, lanes] = (
            total[:, lanes]
            + jnp.dot(more_scr[...], stack[pl.ds(at, more), :], preferred_element_type=F32)
        ).astype(BF16)
    norm = column(jnp.sqrt(own[...] + other[...]))
    s_gate[...] = (jnp.abs(wg[...].astype(F32)) * norm).astype(BF16)
    s_up[...] = (jnp.abs(wu[...].astype(F32)) * norm).astype(BF16)
    half = wg.shape[1]
    norm = column(jnp.sqrt(own_hid[:, 0:half] + other_hid[:, half : 2 * half]))
    s_down[...] = (jnp.abs(wd[...].astype(F32)) * norm).astype(BF16)


def combine(routes, valid, probs, returned, own, other, wg, wu, wd, experts, slots, extra):
    rows, wide = returned.shape
    width = wide - CHUNK
    chunks = width // WIDE
    count, half = routes.shape[1], wg.shape[1]
    small = pl.BlockSpec((routes.shape[0], count), lambda i: (0, 0))
    tall = pl.BlockSpec((WIDE, half), lambda i: (i, 0))
    flat = pl.BlockSpec((half, WIDE), lambda i: (0, i))
    sums = pl.BlockSpec((1, WIDE), lambda i: (0, i))
    last = pl.BlockSpec((1, WIDE), lambda i: (0, chunks))
    return pl.pallas_call(
        functools.partial(combine_kernel, experts, slots, extra, chunks),
        grid=(chunks,),
        in_specs=[
            small, small, small,
            pl.BlockSpec((rows, WIDE), lambda i: (0, i)),
            pl.BlockSpec((rows, CHUNK), lambda i: (0, width // CHUNK)),
            sums, sums, last, last,
            tall, tall, flat,
        ],
        out_specs=[pl.BlockSpec((count, WIDE), lambda i: (0, i)), tall, tall, flat],
        out_shape=[
            jax.ShapeDtypeStruct((count, width), BF16),
            jax.ShapeDtypeStruct(wg.shape, BF16),
            jax.ShapeDtypeStruct(wu.shape, BF16),
            jax.ShapeDtypeStruct(wd.shape, BF16),
        ],
        scratch_shapes=[
            pltpu.VMEM((count, rows), BF16),
            pltpu.VMEM((count, experts * extra), BF16),
            pltpu.VMEM((rows, CHUNK), BF16),
        ],
        compiler_params=pltpu.CompilerParams(vmem_limit_bytes=VMEM),
        cost_estimate=pl.CostEstimate(flops=4 * rows * count * width, bytes_accessed=6 * rows * wide, transcendentals=0),
    )(routes, valid, probs, returned, returned, own, other, own, other, wg, wu, wd)


def swap(value):
    return lax.ppermute(value, "tp", [(0, 1), (1, 0)])


def exchange(value, experts, slots):
    value = value.reshape(experts, slots, value.shape[1])
    value = lax.all_to_all(value, "exp", split_axis=0, concat_axis=0, tiled=True)
    return value.reshape(experts * slots, value.shape[2])


def per_device(tokens, gate_weight, up_weight, down_weight, routes, gate_probs, valid_mask):
    count, top = routes.shape
    experts = lax.axis_size("exp")
    cap = max(2, count * top * 9 // (8 * experts))
    extra = 2
    slots = cap - extra
    w_gate, w_up, w_down = gate_weight[0], up_weight[0], down_weight[0]
    o_gate, o_up = swap(w_gate), swap(w_up)
    routes, valid_mask, gate_probs = routes.T, valid_mask.T, gate_probs.T
    sent = build(routes, valid_mask, gate_probs, tokens, experts, slots, extra)
    received = exchange(after(sent, o_gate, o_up), experts, slots)
    more, w_col, late_down = unpack(received, w_down, experts, slots, extra)
    o_down = swap(late_down)
    hid, sums = hidden_units(received, more, w_col, w_gate, o_gate, w_up, o_up, experts, slots, extra)
    other = swap(sums)
    outs = after(down(hid, w_down, o_down, experts, slots, extra), other)
    returned = exchange(outs, experts, slots)
    mixed, score_gate, score_up, score_down = combine(
        routes, valid_mask, gate_probs, returned, sums, other, w_gate, w_up, w_down, experts, slots, extra
    )
    return (mixed, score_gate[None], score_up[None], score_down[None])


def solution(mesh):
    in_specs = (
        P(("exp", "tp"), None),
        P("exp", None, "tp"),
        P("exp", None, "tp"),
        P("exp", "tp", None),
        P(("exp", "tp"), None),
        P(("exp", "tp"), None),
        P(("exp", "tp"), None),
    )
    out_specs = (
        P(("exp", "tp"), None),
        P("exp", None, "tp"),
        P("exp", None, "tp"),
        P("exp", "tp", None),
    )
    return jax.shard_map(
        per_device, mesh=mesh, in_specs=in_specs, out_specs=out_specs, check_vma=False
    )
```

```python
import functools

import jax
import jax.numpy as jnp
from jax import lax
from jax.experimental import pallas as pl
from jax.experimental.pallas import tpu as pltpu
from jax.sharding import PartitionSpec as P

BF16, F32 = jnp.bfloat16, jnp.float32
CHUNK = 512
WIDE = 1024
HALVES = 2
EXTRA = 1
VMEM = 56 * 1024 * 1024


def iota(shape, dim):
    return lax.broadcasted_iota(jnp.int32, shape, dim)


def one_hot(match):
    return jnp.where(match, 1.0, 0.0).astype(BF16)


def params():
    return pltpu.CompilerParams(vmem_limit_bytes=VMEM)


def by_chunk(blocks, slots):
    more = blocks * EXTRA
    row = iota((blocks * slots, 1), 0)
    home = (row % more) // EXTRA * slots + row // more * EXTRA + row % EXTRA
    return one_hot(home == iota((blocks * slots, blocks * slots), 1))


def by_block(blocks, slots):
    more = blocks * EXTRA
    row = iota((blocks * slots, 1), 0)
    home = row % slots // EXTRA * more + row // slots * EXTRA + row % EXTRA
    return one_hot(home == iota((blocks * slots, blocks * slots), 1))


def assign(experts, routes, valid, probs):
    count = routes.shape[1]
    ids = iota((experts, count), 0)
    named, weight = jnp.zeros((experts, count), F32), jnp.zeros((experts, count), F32)
    for k in range(routes.shape[0]):
        hit = (routes[k : k + 1, :] == ids) & (valid[k : k + 1, :] > 0)
        named = named + jnp.where(hit, 1.0, 0.0)
        weight = weight + jnp.where(hit, probs[k : k + 1, :], 0.0)
    before = one_hot(iota((count, count), 0) < iota((count, count), 1))
    place = jnp.dot(named.astype(BF16), before, preferred_element_type=F32)
    return jnp.where(named > 0, place, -1.0).astype(jnp.int32), weight


def build_kernel(experts, slots, part, chunks, routes, valid, probs, tok, out, slot_scr, sel_scr, stack, w_scr):
    i = pl.program_id(0)
    count = routes.shape[1]
    rows = experts * slots
    row = iota((experts, slots, count), 1)

    @pl.when(i == 0)
    def _():
        slot, weight = assign(experts, routes, valid, probs)
        slot_scr[...] = slot
        slot, weight = slot.reshape(experts, 1, count), weight.reshape(experts, 1, count)
        first = part * (slots + EXTRA)
        sel_scr[...] = jnp.where(slot == row + first, 1.0, 0.0).reshape(rows, count).astype(BF16)
        if part == 0:
            lane = iota((experts, slots, 128), 2)
            packed = jnp.zeros((experts, slots, 128), F32)
            for h in range(HALVES):
                at = h * (slots + EXTRA)
                w_main = jnp.sum(jnp.where(slot == row + at, weight, 0.0), axis=2, keepdims=True)
                w_more = jnp.sum(
                    jnp.where((slot == row + (at + slots)) & (row < EXTRA), weight, 0.0), axis=2, keepdims=True
                )
                packed = jnp.where(lane == 2 * h, w_main, jnp.where(lane == 2 * h + 1, w_more, packed))
            w_scr[...] = packed.reshape(rows, 128).astype(BF16)

    @pl.when(i < chunks)
    def _():
        out[...] = jnp.dot(sel_scr[...], tok[...], preferred_element_type=F32).astype(BF16)
        for p in range(WIDE // CHUNK):
            at = pl.multiple_of((i * (WIDE // CHUNK) + p) * count, count)
            stack[pl.ds(at, count), :] = tok[:, p * CHUNK : (p + 1) * CHUNK]

    @pl.when(i == chunks)
    def _():
        slot = slot_scr[...].reshape(experts, 1, count)
        late = part * (slots + EXTRA) + slots
        wanted = jnp.where(slot == row % EXTRA + late, row // EXTRA, -1).reshape(rows, count)
        pick = jnp.concatenate([one_hot(wanted == c) for c in range(slots // EXTRA)], axis=1)
        out[:, 0:CHUNK] = jnp.dot(pick, stack[...], preferred_element_type=F32).astype(BF16)
        if part == 0:
            out[:, CHUNK : CHUNK + 128] = w_scr[...]


def build(part, routes, valid, probs, tokens, experts, slots):
    count, width = tokens.shape
    chunks = width // WIDE
    rows = experts * slots
    small = pl.BlockSpec((routes.shape[0], count), lambda i: (0, 0))
    return pl.pallas_call(
        functools.partial(build_kernel, experts, slots, part, chunks),
        grid=(chunks + 1,),
        in_specs=[small, small, small, pl.BlockSpec((count, WIDE), lambda i: (0, jnp.minimum(i, chunks - 1)))],
        out_specs=pl.BlockSpec((rows, WIDE), lambda i: (0, i)),
        out_shape=jax.ShapeDtypeStruct((rows, width + CHUNK + (128 if part == 0 else 0)), BF16),
        scratch_shapes=[
            pltpu.VMEM((experts, count), jnp.int32),
            pltpu.VMEM((rows, count), BF16),
            pltpu.VMEM((width // CHUNK * count, CHUNK), BF16),
            pltpu.VMEM((rows, 128), BF16),
        ],
        compiler_params=params(),
        cost_estimate=pl.CostEstimate(flops=4 * rows * count * width, bytes_accessed=2 * rows * width, transcendentals=0),
    )(routes, valid, probs, tokens)


def expert_kernel(blocks, slots, part, chunks, *refs):
    x, x_more, x_w, wg0, wg1, wu0, wu1, wd0, wd1 = refs[:9]
    so_far = refs[9] if part else None
    out, sq, more_scr, w_col, xs, acc0, acc1, hid = refs[10 if part else 9 :]
    i = pl.program_id(0)
    rows, more = blocks * slots, blocks * EXTRA
    half = wg0.shape[1]
    parts = WIDE // CHUNK
    base = lambda lanes: so_far[:, lanes] if part else 0.0

    @pl.when(i == 0)
    def _():
        acc0[...] = jnp.zeros_like(acc0)
        acc1[...] = jnp.zeros_like(acc1)
        pick = by_chunk(blocks, slots)
        more_scr[...] = jnp.dot(pick, x_more[...], preferred_element_type=F32).astype(BF16)
        lane = 2 * part
        w_main = x_w[...].astype(F32)
        w_more = jnp.dot(pick[0:more], x_w[...], preferred_element_type=F32)
        w_col[0:rows, :] = jnp.broadcast_to(w_main[:, lane : lane + 1], (rows, 128))
        w_col[rows : rows + more, :] = jnp.broadcast_to(w_more[:, lane + 1 : lane + 2], (more, 128))

    @pl.when(i < chunks)
    def _():
        xs[0:rows, :] = x[...]
        for p in range(parts):
            at = pl.multiple_of((i * parts + p) * more, more)
            xs[rows : rows + more, p * CHUNK : (p + 1) * CHUNK] = more_scr[pl.ds(at, more), :]
        acc0[...] += jnp.dot(xs[...], jnp.concatenate([wg0[...], wu0[...]], axis=1), preferred_element_type=F32)
        acc1[...] += jnp.dot(xs[...], jnp.concatenate([wg1[...], wu1[...]], axis=1), preferred_element_type=F32)
        for lane in range(0, WIDE, 128):
            lanes = slice(lane, lane + 128)
            value = xs[:, lanes].astype(F32)
            sq[:, lanes] = base(lanes) + jnp.sum(value * value * w_col[...], axis=0, keepdims=True)

    @pl.when(i == chunks)
    def _():
        sq[...] = jnp.zeros_like(sq)
        for at, acc in ((0, acc0), (half, acc1)):
            for lane in range(0, half, 128):
                gate = acc[:, lane : lane + 128]
                up = acc[:, half + lane : half + lane + 128]
                value = (gate / (1.0 + jnp.exp(-gate)) * up).astype(BF16)
                lanes = slice(at + lane, at + lane + 128)
                hid[:, lanes] = value
                value = value.astype(F32)
                sq[:, lanes] = base(lanes) + jnp.sum(value * value * w_col[...], axis=0, keepdims=True)

    @pl.when((i >= chunks) & (i < 2 * chunks))
    def _():
        result = jnp.dot(
            hid[...], jnp.concatenate([wd0[...], wd1[...]], axis=0), preferred_element_type=F32
        ).astype(BF16)
        out[...] = result[0:rows]
        for p in range(parts):
            at = pl.multiple_of(((i - chunks) * parts + p) * more, more)
            more_scr[pl.ds(at, more), :] = result[rows : rows + more, p * CHUNK : (p + 1) * CHUNK]

    @pl.when(i == 2 * chunks)
    def _():
        out[:, 0:CHUNK] = jnp.dot(
            by_block(blocks, slots), more_scr[...], preferred_element_type=F32
        ).astype(BF16)


def expert(part, received, carrier, weights, so_far, blocks, slots):
    width, half = weights[0].shape
    chunks = width // WIDE
    rows, more = blocks * slots, blocks * EXTRA
    up_to = lambda i: jnp.minimum(i, chunks - 1)
    after = lambda i: jnp.clip(i - chunks, 0, chunks - 1)
    w_in = pl.BlockSpec((WIDE, half), lambda i: (up_to(i), 0))
    w_out = pl.BlockSpec((half, WIDE), lambda i: (0, after(i)))
    sums = pl.BlockSpec((1, WIDE), lambda i: (0, jnp.minimum(i, chunks)))
    return pl.pallas_call(
        functools.partial(expert_kernel, blocks, slots, part, chunks),
        grid=(2 * chunks + 1,),
        in_specs=[
            pl.BlockSpec((rows, WIDE), lambda i: (0, up_to(i))),
            pl.BlockSpec((rows, CHUNK), lambda i: (0, width // CHUNK)),
            pl.BlockSpec((rows, 128), lambda i: (0, (width + CHUNK) // 128)),
            w_in, w_in, w_in, w_in, w_out, w_out,
        ] + [sums] * len(so_far),
        out_specs=[pl.BlockSpec((rows, WIDE), lambda i: (0, jnp.maximum(i - chunks, 0))), sums],
        out_shape=[
            jax.ShapeDtypeStruct((rows, width + CHUNK), BF16),
            jax.ShapeDtypeStruct((1, width + WIDE), F32),
        ],
        scratch_shapes=[
            pltpu.VMEM((rows, CHUNK), BF16),
            pltpu.VMEM((rows + more, 128), F32),
            pltpu.VMEM((rows + more, WIDE), BF16),
            pltpu.VMEM((rows + more, 2 * half), F32),
            pltpu.VMEM((rows + more, 2 * half), F32),
            pltpu.VMEM((rows + more, 2 * half), BF16),
        ],
        compiler_params=params(),
        cost_estimate=pl.CostEstimate(
            flops=12 * (rows + more) * width * half, bytes_accessed=4 * rows * width + 12 * width * half, transcendentals=0
        ),
    )(received, received, carrier, *weights, *so_far)


def column(line):
    eye = iota((128, 128), 0) == iota((128, 128), 1)
    return jnp.concatenate(
        [
            jnp.sum(jnp.where(eye, line[:, at : at + 128], 0.0), axis=1, keepdims=True)
            for at in range(0, line.shape[1], 128)
        ],
        axis=0,
    )


def combine_kernel(experts, slots, part, *refs):
    routes, valid, probs, x, x_more = refs[:5]
    if part:
        so_far, out, sel_scr, more_scr, stack = refs[5:]
    else:
        own, other, own_hid, other_hid, wg, wu, wd, out, s_gate, s_up, s_down, sel_scr, more_scr, stack = refs[5:]
    i = pl.program_id(0)
    count = routes.shape[1]
    rows, more = experts * slots, experts * EXTRA

    @pl.when(i == 0)
    def _():
        slot, weight = assign(experts, routes, valid, probs)
        slot, weight = slot.reshape(experts, 1, count), weight.reshape(experts, 1, count)
        first = part * (slots + EXTRA)
        hits = slot == iota((experts, slots, count), 1) + first
        sel_scr[...] = jnp.where(hits, weight, 0.0).reshape(rows, count).T.astype(BF16)
        spread = jnp.zeros((more, count), F32)
        for r in range(EXTRA):
            late = jnp.where(slot == first + slots + r, weight, 0.0).reshape(experts, count)
            widen = one_hot(iota((more, experts), 0) == iota((more, experts), 1) * EXTRA + r)
            spread = spread + jnp.dot(widen, late.astype(BF16), preferred_element_type=F32)
        more_scr[...] = spread.T.astype(BF16)
        stack[...] = jnp.dot(by_chunk(experts, slots), x_more[...], preferred_element_type=F32).astype(BF16)

    total = jnp.dot(sel_scr[...], x[...], preferred_element_type=F32)
    if part:
        total = total + so_far[...]
    for p in range(WIDE // CHUNK):
        at = pl.multiple_of((i * (WIDE // CHUNK) + p) * more, more)
        lanes = slice(p * CHUNK, (p + 1) * CHUNK)
        out[:, lanes] = (
            total[:, lanes] + jnp.dot(more_scr[...], stack[pl.ds(at, more), :], preferred_element_type=F32)
        ).astype(out.dtype)
    if not part:
        half = wg.shape[1]
        norm = column(jnp.sqrt(own[...] + other[...]))
        s_gate[...] = (jnp.abs(wg[...].astype(F32)) * norm).astype(BF16)
        s_up[...] = (jnp.abs(wu[...].astype(F32)) * norm).astype(BF16)
        norm = column(jnp.sqrt(own_hid[:, 0:half] + other_hid[:, half : 2 * half]))
        s_down[...] = (jnp.abs(wd[...].astype(F32)) * norm).astype(BF16)


def combine(part, routes, valid, probs, returned, experts, slots, so_far=None, own=None, other=None, weights=None):
    rows, wide = returned.shape
    width = wide - CHUNK
    chunks = width // WIDE
    count = routes.shape[1]
    small = pl.BlockSpec((routes.shape[0], count), lambda i: (0, 0))
    whole = pl.BlockSpec((count, WIDE), lambda i: (0, i))
    in_specs = [
        small, small, small,
        pl.BlockSpec((rows, WIDE), lambda i: (0, i)),
        pl.BlockSpec((rows, CHUNK), lambda i: (0, width // CHUNK)),
    ]
    if part:
        in_specs, out_specs = in_specs + [whole], whole
        out_shape = jax.ShapeDtypeStruct((count, width), BF16)
        given = (so_far,)
    else:
        half = weights[0].shape[1]
        tall = pl.BlockSpec((WIDE, half), lambda i: (i, 0))
        flat = pl.BlockSpec((half, WIDE), lambda i: (0, i))
        sums = pl.BlockSpec((1, WIDE), lambda i: (0, i))
        last = pl.BlockSpec((1, WIDE), lambda i: (0, chunks))
        in_specs = in_specs + [sums, sums, last, last, tall, tall, flat]
        out_specs = [whole, tall, tall, flat]
        out_shape = [jax.ShapeDtypeStruct((count, width), F32)] + [jax.ShapeDtypeStruct(w.shape, BF16) for w in weights]
        given = (own, other, own, other) + tuple(weights)
    return pl.pallas_call(
        functools.partial(combine_kernel, experts, slots, part),
        grid=(chunks,),
        in_specs=in_specs,
        out_specs=out_specs,
        out_shape=out_shape,
        scratch_shapes=[
            pltpu.VMEM((count, rows), BF16),
            pltpu.VMEM((count, experts * EXTRA), BF16),
            pltpu.VMEM((rows, CHUNK), BF16),
        ],
        compiler_params=params(),
        cost_estimate=pl.CostEstimate(flops=4 * rows * count * width, bytes_accessed=6 * rows * wide, transcendentals=0),
    )(routes, valid, probs, returned, returned, *given)


def swap(value):
    return lax.ppermute(value, "tp", [(0, 1), (1, 0)])


def exchange(value, experts, slots):
    value = value.reshape(experts, slots, value.shape[1])
    value = lax.all_to_all(value, "exp", split_axis=0, concat_axis=0, tiled=True)
    return value.reshape(experts * slots, value.shape[2])


def per_device(tokens, gate_weight, up_weight, down_weight, routes, gate_probs, valid_mask):
    count, top = routes.shape
    experts = lax.axis_size("exp")
    cap = max(2, count * top * 9 // (8 * experts))
    slots = cap // HALVES - EXTRA
    own = gate_weight[0], up_weight[0], down_weight[0]
    weights = [w for mine in own for w in (mine, swap(mine))]
    routing = routes.T, valid_mask.T, gate_probs.T
    sent = [build(part, *routing, tokens, experts, slots) for part in range(HALVES)]
    received = [exchange(half, experts, slots) for half in sent]
    outs0, sums = expert(0, received[0], received[0], weights, (), experts, slots)
    outs1, sums = expert(1, received[1], received[0], weights, (sums,), experts, slots)
    returned = [exchange(half, experts, slots) for half in (outs0, outs1)]
    mixed, score_gate, score_up, score_down = combine(
        0, *routing, returned[0], experts, slots, own=sums, other=swap(sums), weights=own
    )
    mixed = combine(1, *routing, returned[1], experts, slots, so_far=mixed)
    return (mixed, score_gate[None], score_up[None], score_down[None])


def solution(mesh):
    in_specs = (
        P(("exp", "tp"), None),
        P("exp", None, "tp"),
        P("exp", None, "tp"),
        P("exp", "tp", None),
        P(("exp", "tp"), None),
        P(("exp", "tp"), None),
        P(("exp", "tp"), None),
    )
    out_specs = (
        P(("exp", "tp"), None),
        P("exp", None, "tp"),
        P("exp", None, "tp"),
        P("exp", "tp", None),
    )
    return jax.shard_map(
        per_device, mesh=mesh, in_specs=in_specs, out_specs=out_specs, check_vma=False
    )
```

```python
import functools

import jax
import jax.numpy as jnp
from jax import lax
from jax.experimental import pallas as pl
from jax.experimental.pallas import tpu as pltpu
from jax.sharding import PartitionSpec as P

BF16, F32 = jnp.bfloat16, jnp.float32
CHUNK = 512
WIDE = 1024
PIECES = 3
VMEM = 56 * 1024 * 1024


def iota(shape, dim):
    return lax.broadcasted_iota(jnp.int32, shape, dim)


def one_hot(match):
    return jnp.where(match, 1.0, 0.0).astype(BF16)


def planes(width):
    return [(plane, slice(plane * 128, (plane + 1) * 128)) for plane in range(width // 128)]


def to_chunks(wide, packed, by_chunk, blocks, slots):
    for plane, lanes in planes(CHUNK):
        wide[plane] = packed[:, lanes].astype(F32)
        for at in range(slots):
            picked = wide[plane, pl.ds(at, blocks, stride=slots), :]
            by_chunk[at * blocks : (at + 1) * blocks, lanes] = picked.astype(BF16)


def to_blocks(wide, by_chunk, packed, blocks, slots):
    for plane, lanes in planes(CHUNK):
        for at in range(slots):
            rows = by_chunk[at * blocks : (at + 1) * blocks, lanes]
            wide[plane, pl.ds(at, blocks, stride=slots), :] = rows.astype(F32)
        packed[:, lanes] = wide[plane].astype(BF16)


def assign(experts, routes, valid, probs):
    count = routes.shape[1]
    ids = iota((experts, count), 0)
    named, weight = jnp.zeros((experts, count), F32), jnp.zeros((experts, count), F32)
    for k in range(routes.shape[0]):
        hit = (routes[k : k + 1, :] == ids) & (valid[k : k + 1, :] > 0)
        named = named + jnp.where(hit, 1.0, 0.0)
        weight = weight + jnp.where(hit, probs[k : k + 1, :], 0.0)
    before = one_hot(iota((count, count), 0) < iota((count, count), 1))
    place = jnp.dot(named.astype(BF16), before, preferred_element_type=F32)
    return jnp.where(named > 0, place, -1.0).astype(jnp.int32), weight


def build_kernel(experts, slots, extra, chunks, routes, valid, probs, tok, out, back, back_more, sel_scr, pick_scr, stack, wide, w_scr):
    i = pl.program_id(0)
    more = experts * extra
    count = routes.shape[1]
    rows = experts * slots
    row = iota((experts, slots, count), 1)

    @pl.when(i == 0)
    def _():
        slot, weight = assign(experts, routes, valid, probs)
        slot, weight = slot.reshape(experts, 1, count), weight.reshape(experts, 1, count)
        hits = slot == row
        sel_scr[...] = jnp.where(hits, 1.0, 0.0).reshape(rows, count).astype(BF16)
        w_main = jnp.sum(jnp.where(hits, weight, 0.0), axis=2, keepdims=True)
        w_more = jnp.sum(jnp.where((slot == row + slots) & (row < extra), weight, 0.0), axis=2, keepdims=True)
        lane = iota((experts, slots, 128), 2)
        packed = jnp.where(lane == 0, w_main, jnp.where(lane == 1, w_more, 0.0))
        w_scr[...] = packed.reshape(rows, 128).astype(BF16)
        back[...] = jnp.where(hits, weight, 0.0).reshape(rows, count).T.astype(BF16)
        for r in range(extra):
            late = (slot == slots + r).reshape(experts, count)
            pick_scr[r * experts : (r + 1) * experts, :] = jnp.where(late, 1.0, 0.0).astype(BF16)
        late = [jnp.where(slot == slots + r, weight, 0.0).reshape(experts, count) for r in range(extra)]
        back_more[...] = jnp.concatenate(late, axis=0).T.astype(BF16)

    @pl.when(i < chunks)
    def _():
        out[...] = jnp.dot(sel_scr[...], tok[...], preferred_element_type=F32).astype(BF16)
        late = jnp.dot(pick_scr[...], tok[...], preferred_element_type=F32).astype(BF16)
        for part in range(WIDE // CHUNK):
            at = pl.multiple_of((i * (WIDE // CHUNK) + part) * more, more)
            stack[pl.ds(at, more), :] = late[:, part * CHUNK : (part + 1) * CHUNK]

    @pl.when(i == chunks)
    def _():
        to_blocks(wide, stack, out, experts, slots)
        out[:, CHUNK : CHUNK + 128] = w_scr[...]


def build(routes, valid, probs, tokens, experts, slots, extra):
    count, width = tokens.shape
    chunks = width // WIDE
    rows = experts * slots
    small = pl.BlockSpec((routes.shape[0], count), lambda i: (0, 0))
    return pl.pallas_call(
        functools.partial(build_kernel, experts, slots, extra, chunks),
        grid=(chunks + 1,),
        in_specs=[small, small, small, pl.BlockSpec((count, WIDE), lambda i: (0, jnp.minimum(i, chunks - 1)))],
        out_specs=[
            pl.BlockSpec((rows, WIDE), lambda i: (0, i)),
            pl.BlockSpec((count, rows), lambda i: (0, 0)),
            pl.BlockSpec((count, experts * extra), lambda i: (0, 0)),
        ],
        out_shape=[
            jax.ShapeDtypeStruct((rows, width + CHUNK + 128), BF16),
            jax.ShapeDtypeStruct((count, rows), BF16),
            jax.ShapeDtypeStruct((count, experts * extra), BF16),
        ],
        scratch_shapes=[
            pltpu.VMEM((rows, count), BF16),
            pltpu.VMEM((experts * extra, count), BF16),
            pltpu.VMEM((rows, CHUNK), BF16),
            pltpu.VMEM((CHUNK // 128, rows, 128), F32),
            pltpu.VMEM((rows, 128), BF16),
        ],
        compiler_params=pltpu.CompilerParams(vmem_limit_bytes=VMEM),
        cost_estimate=pl.CostEstimate(flops=4 * rows * count * width, bytes_accessed=2 * rows * width, transcendentals=0),
    )(routes, valid, probs, tokens)


def copy_kernel(given, first, copied, held, sem_in, sem_out):
    count = held.shape[0]
    pieces = [pl.ds(at * WIDE, WIDE) for at in range(count)]
    ins = [pltpu.make_async_copy(given.at[:, p], held.at[at], sem_in.at[at]) for at, p in enumerate(pieces)]
    outs = [pltpu.make_async_copy(held.at[at], copied.at[:, p], sem_out.at[at]) for at, p in enumerate(pieces)]
    for copy in ins:
        copy.start()
    for at in range(count):
        ins[at].wait()
        outs[at].start()
    for copy in outs:
        copy.wait()


def copy_after(value, first):
    high, width = value.shape
    count = width // WIDE
    anywhere = pl.BlockSpec(memory_space=pl.ANY)
    return pl.pallas_call(
        copy_kernel,
        in_specs=[anywhere, anywhere],
        out_specs=anywhere,
        out_shape=jax.ShapeDtypeStruct(value.shape, value.dtype),
        scratch_shapes=[
            pltpu.VMEM((count, high, WIDE), value.dtype),
            pltpu.SemaphoreType.DMA((count,)),
            pltpu.SemaphoreType.DMA((count,)),
        ],
        compiler_params=pltpu.CompilerParams(vmem_limit_bytes=VMEM),
        cost_estimate=pl.CostEstimate(flops=0, bytes_accessed=4 * high * width, transcendentals=0),
    )(value, first)


def hidden_kernel(blocks, slots, extra, chunks, x, x_more, x_w, wg0, wg1, wu0, wu1, hid, sq, xs, acc0, acc1, w_col,
                  wide, late):
    i = pl.program_id(0)
    rows, more = blocks * slots, blocks * extra
    half = wg0.shape[1]
    parts = WIDE // CHUNK

    def fill():
        xs[0:rows, :] = x[...]
        for part in range(parts):
            at = pl.multiple_of((i * parts + part) * more, more)
            xs[rows : rows + more, part * CHUNK : (part + 1) * CHUNK] = late[pl.ds(at, more), :]

    def squares():
        for lane in range(0, WIDE, 128):
            part = xs[:, lane : lane + 128].astype(F32)
            sq[:, lane : lane + 128] = jnp.sum(part * part * w_col[...], axis=0, keepdims=True)

    def products(at, high):
        piece = xs[at : at + high, :]
        return (
            jnp.dot(piece, jnp.concatenate([wg0[...], wu0[...]], axis=1), preferred_element_type=F32),
            jnp.dot(piece, jnp.concatenate([wg1[...], wu1[...]], axis=1), preferred_element_type=F32),
        )

    @pl.when(i == 0)
    def _():
        wide[0] = x_w[...].astype(F32)
        w_col[0:rows, :] = jnp.broadcast_to(wide[0, :, 0:1], (rows, 128))
        for r in range(extra):
            w_more = wide[0, pl.ds(r, blocks, stride=slots), :]
            w_col[rows + r * blocks : rows + (r + 1) * blocks, :] = jnp.broadcast_to(w_more[:, 1:2], (blocks, 128))
        to_chunks(wide, x_more, late, blocks, slots)
        fill()
        acc0[...], acc1[...] = products(0, rows + more)
        squares()

    @pl.when((i > 0) & (i < chunks - 1))
    def _():
        fill()
        first, second = products(0, rows + more)
        acc0[...] += first
        acc1[...] += second
        squares()

    @pl.when(i == chunks - 1)
    def _():
        fill()
        squares()
        high = (rows + more) // PIECES
        for at in range(0, rows + more, high):
            span = slice(at, at + high)
            for start, acc, product in zip((0, half), (acc0, acc1), products(at, high)):
                gate = acc[span, 0:half] + product[:, 0:half]
                up = acc[span, half : 2 * half] + product[:, half : 2 * half]
                hid[span, start : start + half] = (gate * (0.5 + 0.5 * jnp.tanh(0.5 * gate)) * up).astype(BF16)

    @pl.when(i == chunks)
    def _():
        sq[...] = jnp.zeros_like(sq)
        for lane in range(0, 2 * half, 128):
            value = hid[:, lane : lane + 128].astype(F32)
            sq[:, lane : lane + 128] = jnp.sum(value * value * w_col[...], axis=0, keepdims=True)


def hidden_units(received, wg0, wg1, wu0, wu1, blocks, slots, extra):
    width, half = wg0.shape
    chunks = width // WIDE
    rows, more = blocks * slots, blocks * extra
    up_to = lambda i: jnp.minimum(i, chunks - 1)
    w_in = pl.BlockSpec((WIDE, half), lambda i: (up_to(i), 0))
    return pl.pallas_call(
        functools.partial(hidden_kernel, blocks, slots, extra, chunks),
        grid=(chunks + 1,),
        in_specs=[
            pl.BlockSpec((rows, WIDE), lambda i: (0, up_to(i))),
            pl.BlockSpec((rows, CHUNK), lambda i: (0, width // CHUNK)),
            pl.BlockSpec((rows, 128), lambda i: (0, (width + CHUNK) // 128)),
            w_in, w_in, w_in, w_in,
        ],
        out_specs=[
            pl.BlockSpec((rows + more, 2 * half), lambda i: (0, 0)),
            pl.BlockSpec((1, WIDE), lambda i: (0, i)),
        ],
        out_shape=[
            jax.ShapeDtypeStruct((rows + more, 2 * half), BF16),
            jax.ShapeDtypeStruct((1, width + WIDE), F32),
        ],
        scratch_shapes=[
            pltpu.VMEM((rows + more, WIDE), BF16),
            pltpu.VMEM((rows + more, 2 * half), F32),
            pltpu.VMEM((rows + more, 2 * half), F32),
            pltpu.VMEM((rows + more, 128), F32),
            pltpu.VMEM((CHUNK // 128, rows, 128), F32),
            pltpu.VMEM((rows, CHUNK), BF16),
        ],
        compiler_params=pltpu.CompilerParams(vmem_limit_bytes=VMEM),
        cost_estimate=pl.CostEstimate(
            flops=8 * (rows + more) * width * half, bytes_accessed=2 * rows * width + 8 * width * half, transcendentals=0
        ),
    )(received, received, received, wg0, wg1, wu0, wu1)


def down_kernel(blocks, slots, extra, chunks, hid, wd0, wd1, out, stack, wide):
    i = pl.program_id(0)
    rows, more = blocks * slots, blocks * extra
    parts = WIDE // CHUNK

    @pl.when(i < chunks)
    def _():
        result = jnp.dot(
            hid[...], jnp.concatenate([wd0[...], wd1[...]], axis=0), preferred_element_type=F32
        ).astype(BF16)
        out[...] = result[0:rows]
        for part in range(parts):
            at = pl.multiple_of((i * parts + part) * more, more)
            stack[pl.ds(at, more), :] = result[rows : rows + more, part * CHUNK : (part + 1) * CHUNK]

    @pl.when(i == chunks)
    def _():
        to_blocks(wide, stack, out, blocks, slots)


def down(hid, wd0, wd1, blocks, slots, extra):
    half, width = wd0.shape
    chunks = width // WIDE
    rows = blocks * slots
    w_out = pl.BlockSpec((half, WIDE), lambda i: (0, jnp.minimum(i, chunks - 1)))
    return pl.pallas_call(
        functools.partial(down_kernel, blocks, slots, extra, chunks),
        grid=(chunks + 1,),
        in_specs=[pl.BlockSpec(hid.shape, lambda i: (0, 0)), w_out, w_out],
        out_specs=pl.BlockSpec((rows, WIDE), lambda i: (0, i)),
        out_shape=jax.ShapeDtypeStruct((rows, width + CHUNK), BF16),
        scratch_shapes=[pltpu.VMEM((rows, CHUNK), BF16), pltpu.VMEM((CHUNK // 128, rows, 128), F32)],
        compiler_params=pltpu.CompilerParams(vmem_limit_bytes=VMEM),
        cost_estimate=pl.CostEstimate(
            flops=4 * hid.shape[0] * width * half, bytes_accessed=2 * rows * width + 4 * width * half, transcendentals=0
        ),
    )(hid, wd0, wd1)


def after(value, *first):
    anywhere = pl.BlockSpec(memory_space=pl.ANY)
    return pl.pallas_call(
        lambda *refs: None,
        in_specs=[anywhere] * (1 + len(first)),
        out_specs=anywhere,
        out_shape=jax.ShapeDtypeStruct(value.shape, value.dtype),
        input_output_aliases={0: 0},
        cost_estimate=pl.CostEstimate(flops=0, bytes_accessed=0, transcendentals=0),
    )(value, *first)


def column(line):
    eye = iota((128, 128), 0) == iota((128, 128), 1)
    return jnp.concatenate(
        [
            jnp.sum(jnp.where(eye, line[:, at : at + 128], 0.0), axis=1, keepdims=True)
            for at in range(0, line.shape[1], 128)
        ],
        axis=0,
    )


def combine_kernel(experts, slots, extra, back, back_more, x, x_more, own, other, own_hid, other_hid, wg, wu, wd,
                   out, s_gate, s_up, s_down, wide, late):
    i = pl.program_id(0)
    more, parts = experts * extra, WIDE // CHUNK

    @pl.when(i == 0)
    def _():
        to_chunks(wide, x_more, late, experts, slots)

    total = jnp.dot(back[...], x[...], preferred_element_type=F32)
    for part in range(parts):
        lanes = slice(part * CHUNK, (part + 1) * CHUNK)
        at = pl.multiple_of((i * parts + part) * more, more)
        out[:, lanes] = (
            total[:, lanes] + jnp.dot(back_more[...], late[pl.ds(at, more), :], preferred_element_type=F32)
        ).astype(BF16)
    norm = column(jnp.sqrt(own[...] + other[...]))
    s_gate[...] = (jnp.abs(wg[...].astype(F32)) * norm).astype(BF16)
    s_up[...] = (jnp.abs(wu[...].astype(F32)) * norm).astype(BF16)
    half = wg.shape[1]
    norm = column(jnp.sqrt(own_hid[:, 0:half] + other_hid[:, half : 2 * half]))
    s_down[...] = (jnp.abs(wd[...].astype(F32)) * norm).astype(BF16)


def combine(back, back_more, returned, own, other, wg, wu, wd, experts, slots, extra):
    rows, wide = returned.shape
    width = wide - CHUNK
    chunks = width // WIDE
    count, half = back.shape[0], wg.shape[1]
    tall = pl.BlockSpec((WIDE, half), lambda i: (i, 0))
    flat = pl.BlockSpec((half, WIDE), lambda i: (0, i))
    sums = pl.BlockSpec((1, WIDE), lambda i: (0, i))
    last = pl.BlockSpec((1, WIDE), lambda i: (0, chunks))
    return pl.pallas_call(
        functools.partial(combine_kernel, experts, slots, extra),
        grid=(chunks,),
        in_specs=[
            pl.BlockSpec(back.shape, lambda i: (0, 0)),
            pl.BlockSpec(back_more.shape, lambda i: (0, 0)),
            pl.BlockSpec((rows, WIDE), lambda i: (0, i)),
            pl.BlockSpec((rows, CHUNK), lambda i: (0, width // CHUNK)),
            sums, sums, last, last,
            tall, tall, flat,
        ],
        out_specs=[pl.BlockSpec((count, WIDE), lambda i: (0, i)), tall, tall, flat],
        out_shape=[
            jax.ShapeDtypeStruct((count, width), BF16),
            jax.ShapeDtypeStruct(wg.shape, BF16),
            jax.ShapeDtypeStruct(wu.shape, BF16),
            jax.ShapeDtypeStruct(wd.shape, BF16),
        ],
        scratch_shapes=[pltpu.VMEM((CHUNK // 128, rows, 128), F32), pltpu.VMEM((rows, CHUNK), BF16)],
        compiler_params=pltpu.CompilerParams(vmem_limit_bytes=VMEM),
        cost_estimate=pl.CostEstimate(flops=4 * rows * count * width, bytes_accessed=6 * rows * wide, transcendentals=0),
    )(back, back_more, returned, returned, own, other, own, other, wg, wu, wd)


def swap(value):
    return lax.ppermute(value, "tp", [(0, 1), (1, 0)])


def exchange(value, experts, slots):
    value = value.reshape(experts, slots, value.shape[1])
    value = lax.all_to_all(value, "exp", split_axis=0, concat_axis=0, tiled=True)
    return value.reshape(experts * slots, value.shape[2])


def per_device(tokens, gate_weight, up_weight, down_weight, routes, gate_probs, valid_mask):
    count, top = routes.shape
    experts = lax.axis_size("exp")
    cap = max(2, count * top * 9 // (8 * experts))
    extra = 2
    slots = cap - extra
    w_gate, w_up, w_down = gate_weight[0], up_weight[0], down_weight[0]
    o_gate, o_up = swap(w_gate), swap(w_up)
    routes, valid_mask, gate_probs = routes.T, valid_mask.T, gate_probs.T
    sent, back, back_more = build(routes, valid_mask, gate_probs, tokens, experts, slots, extra)
    received = exchange(after(sent, o_gate, o_up), experts, slots)
    o_down = swap(copy_after(w_down, received))
    hid, sums = hidden_units(received, w_gate, o_gate, w_up, o_up, experts, slots, extra)
    other = swap(sums)
    outs = after(down(hid, w_down, o_down, experts, slots, extra), other)
    returned = exchange(outs, experts, slots)
    mixed, score_gate, score_up, score_down = combine(
        back, back_more, returned, sums, other, w_gate, w_up, w_down, experts, slots, extra
    )
    return (mixed, score_gate[None], score_up[None], score_down[None])


def solution(mesh):
    in_specs = (
        P(("exp", "tp"), None),
        P("exp", None, "tp"),
        P("exp", None, "tp"),
        P("exp", "tp", None),
        P(("exp", "tp"), None),
        P(("exp", "tp"), None),
        P(("exp", "tp"), None),
    )
    out_specs = (
        P(("exp", "tp"), None),
        P("exp", None, "tp"),
        P("exp", None, "tp"),
        P("exp", "tp", None),
    )
    return jax.shard_map(
        per_device, mesh=mesh, in_specs=in_specs, out_specs=out_specs, check_vma=False
    )
```

```python
import functools

import jax
import jax.numpy as jnp
from jax import lax
from jax.experimental import pallas as pl
from jax.experimental.pallas import tpu as pltpu
from jax.sharding import PartitionSpec as P

BF16, F32 = jnp.bfloat16, jnp.float32
CHUNK = 512
WIDE = 1024
PIECES = 8
DOWN_PIECES = 2
NARROW = 1024
VMEM = 56 * 1024 * 1024


def iota(shape, dim):
    return lax.broadcasted_iota(jnp.int32, shape, dim)


def one_hot(match):
    return jnp.where(match, 1.0, 0.0).astype(BF16)


def planes(width):
    return [(plane, slice(plane * 128, (plane + 1) * 128)) for plane in range(width // 128)]


def to_chunks(wide, packed, by_chunk, blocks, slots):
    for plane, lanes in planes(CHUNK):
        wide[plane] = packed[:, lanes].astype(F32)
        for at in range(slots):
            picked = wide[plane, pl.ds(at, blocks, stride=slots), :]
            by_chunk[at * blocks : (at + 1) * blocks, lanes] = picked.astype(BF16)


def to_blocks(wide, by_chunk, packed, blocks, slots):
    for plane, lanes in planes(CHUNK):
        for at in range(slots):
            rows = by_chunk[at * blocks : (at + 1) * blocks, lanes]
            wide[plane, pl.ds(at, blocks, stride=slots), :] = rows.astype(F32)
        packed[:, lanes] = wide[plane].astype(BF16)


def assign(experts, routes, valid, probs):
    count = routes.shape[1]
    ids = iota((experts, count), 0)
    named, weight = jnp.zeros((experts, count), F32), jnp.zeros((experts, count), F32)
    for k in range(routes.shape[0]):
        hit = (routes[k : k + 1, :] == ids) & (valid[k : k + 1, :] > 0)
        named = named + jnp.where(hit, 1.0, 0.0)
        weight = weight + jnp.where(hit, probs[k : k + 1, :], 0.0)
    before = one_hot(iota((count, count), 0) < iota((count, count), 1))
    place = jnp.dot(named.astype(BF16), before, preferred_element_type=F32)
    return jnp.where(named > 0, place, -1.0).astype(jnp.int32), weight


def build_kernel(experts, slots, extra, chunks, routes, valid, probs, tok, wd, out, back, back_more, wd_copy, sel_scr, pick_scr, stack, wide, w_scr):
    i = pl.program_id(0)
    more = experts * extra
    count = routes.shape[1]
    rows = experts * slots
    row = iota((experts, slots, count), 1)

    @pl.when(i == 0)
    def _():
        slot, weight = assign(experts, routes, valid, probs)
        slot, weight = slot.reshape(experts, 1, count), weight.reshape(experts, 1, count)
        hits = slot == row
        sel_scr[...] = jnp.where(hits, 1.0, 0.0).reshape(rows, count).astype(BF16)
        w_main = jnp.sum(jnp.where(hits, weight, 0.0), axis=2, keepdims=True)
        w_more = jnp.sum(jnp.where((slot == row + slots) & (row < extra), weight, 0.0), axis=2, keepdims=True)
        lane = iota((experts, slots, 128), 2)
        packed = jnp.where(lane == 0, w_main, jnp.where(lane == 1, w_more, 0.0))
        w_scr[...] = packed.reshape(rows, 128).astype(BF16)
        back[...] = jnp.where(hits, weight, 0.0).reshape(rows, count).T.astype(BF16)
        for r in range(extra):
            late = (slot == slots + r).reshape(experts, count)
            pick_scr[r * experts : (r + 1) * experts, :] = jnp.where(late, 1.0, 0.0).astype(BF16)
        late = [jnp.where(slot == slots + r, weight, 0.0).reshape(experts, count) for r in range(extra)]
        back_more[...] = jnp.concatenate(late, axis=0).T.astype(BF16)

    @pl.when(i < chunks)
    def _():
        wd_copy[...] = wd[...]
        out[...] = jnp.dot(sel_scr[...], tok[...], preferred_element_type=F32).astype(BF16)
        late = jnp.dot(pick_scr[...], tok[...], preferred_element_type=F32).astype(BF16)
        for part in range(WIDE // CHUNK):
            at = pl.multiple_of((i * (WIDE // CHUNK) + part) * more, more)
            stack[pl.ds(at, more), :] = late[:, part * CHUNK : (part + 1) * CHUNK]

    @pl.when(i == chunks)
    def _():
        to_blocks(wide, stack, out, experts, slots)
        out[:, CHUNK : CHUNK + 128] = w_scr[...]


def build(routes, valid, probs, tokens, wd, experts, slots, extra):
    count, width = tokens.shape
    chunks = width // WIDE
    rows = experts * slots
    small = pl.BlockSpec((routes.shape[0], count), lambda i: (0, 0))
    flat = pl.BlockSpec((wd.shape[0], WIDE), lambda i: (0, jnp.minimum(i, chunks - 1)))
    return pl.pallas_call(
        functools.partial(build_kernel, experts, slots, extra, chunks),
        grid=(chunks + 1,),
        in_specs=[small, small, small, pl.BlockSpec((count, WIDE), lambda i: (0, jnp.minimum(i, chunks - 1))), flat],
        out_specs=[
            pl.BlockSpec((rows, WIDE), lambda i: (0, i)),
            pl.BlockSpec((count, rows), lambda i: (0, 0)),
            pl.BlockSpec((count, experts * extra), lambda i: (0, 0)),
            flat,
        ],
        out_shape=[
            jax.ShapeDtypeStruct((rows, width + CHUNK + 128), BF16),
            jax.ShapeDtypeStruct((count, rows), BF16),
            jax.ShapeDtypeStruct((count, experts * extra), BF16),
            jax.ShapeDtypeStruct(wd.shape, BF16),
        ],
        scratch_shapes=[
            pltpu.VMEM((rows, count), BF16),
            pltpu.VMEM((experts * extra, count), BF16),
            pltpu.VMEM((rows, CHUNK), BF16),
            pltpu.VMEM((CHUNK // 128, rows, 128), F32),
            pltpu.VMEM((rows, 128), BF16),
        ],
        compiler_params=pltpu.CompilerParams(vmem_limit_bytes=VMEM),
        cost_estimate=pl.CostEstimate(flops=4 * rows * count * width, bytes_accessed=2 * rows * width, transcendentals=0),
    )(routes, valid, probs, tokens, wd)


def hidden_kernel(blocks, slots, extra, chunks, x, x_more, x_w, wg0, wg1, wu0, wu1, hid, sq, xs, acc0, acc1, w_col,
                  wide, late):
    i = pl.program_id(0)
    rows, more = blocks * slots, blocks * extra
    half = wg0.shape[1]
    parts = WIDE // CHUNK

    def fill():
        xs[0:rows, :] = x[...]
        for part in range(parts):
            at = pl.multiple_of((i * parts + part) * more, more)
            xs[rows : rows + more, part * CHUNK : (part + 1) * CHUNK] = late[pl.ds(at, more), :]

    def squares(lane):
        part = xs[:, lane : lane + 128].astype(F32)
        sq[:, lane : lane + 128] = jnp.sum(part * part * w_col[...], axis=0, keepdims=True)

    def products(use):
        high = (rows + more) // PIECES
        share = WIDE // PIECES
        for piece in range(PIECES):
            span = slice(piece * high, (piece + 1) * high)
            value = xs[span, :]
            for start, acc, gate, up in ((0, acc0, wg0, wu0), (half, acc1, wg1, wu1)):
                use(span, start, acc, jnp.dot(
                    value, jnp.concatenate([gate[...], up[...]], axis=1), preferred_element_type=F32
                ))
            for lane in range(piece * share, (piece + 1) * share, 128):
                squares(lane)

    def put(span, start, acc, product):
        acc[span, :] = product

    def add(span, start, acc, product):
        acc[span, :] += product

    def finish(span, start, acc, product):
        gate = acc[span, 0:half] + product[:, 0:half]
        up = acc[span, half : 2 * half] + product[:, half : 2 * half]
        hid[span, start : start + half] = (gate * (0.5 + 0.5 * jnp.tanh(0.5 * gate)) * up).astype(BF16)

    @pl.when(i == 0)
    def _():
        wide[0] = x_w[...].astype(F32)
        w_col[0:rows, :] = jnp.broadcast_to(wide[0, :, 0:1], (rows, 128))
        for r in range(extra):
            w_more = wide[0, pl.ds(r, blocks, stride=slots), :]
            w_col[rows + r * blocks : rows + (r + 1) * blocks, :] = jnp.broadcast_to(w_more[:, 1:2], (blocks, 128))
        to_chunks(wide, x_more, late, blocks, slots)
        fill()
        products(put)

    @pl.when((i > 0) & (i < chunks - 1))
    def _():
        fill()
        products(add)

    @pl.when(i == chunks - 1)
    def _():
        fill()
        products(finish)

    @pl.when(i == chunks)
    def _():
        sq[...] = jnp.zeros_like(sq)
        for lane in range(0, 2 * half, 128):
            value = hid[:, lane : lane + 128].astype(F32)
            sq[:, lane : lane + 128] = jnp.sum(value * value * w_col[...], axis=0, keepdims=True)


def hidden_units(received, wg0, wg1, wu0, wu1, blocks, slots, extra):
    width, half = wg0.shape
    chunks = width // WIDE
    rows, more = blocks * slots, blocks * extra
    up_to = lambda i: jnp.minimum(i, chunks - 1)
    w_in = pl.BlockSpec((WIDE, half), lambda i: (up_to(i), 0))
    return pl.pallas_call(
        functools.partial(hidden_kernel, blocks, slots, extra, chunks),
        grid=(chunks + 1,),
        in_specs=[
            pl.BlockSpec((rows, WIDE), lambda i: (0, up_to(i))),
            pl.BlockSpec((rows, CHUNK), lambda i: (0, width // CHUNK)),
            pl.BlockSpec((rows, 128), lambda i: (0, (width + CHUNK) // 128)),
            w_in, w_in, w_in, w_in,
        ],
        out_specs=[
            pl.BlockSpec((rows + more, 2 * half), lambda i: (0, 0)),
            pl.BlockSpec((1, WIDE), lambda i: (0, i)),
        ],
        out_shape=[
            jax.ShapeDtypeStruct((rows + more, 2 * half), BF16),
            jax.ShapeDtypeStruct((1, width + WIDE), F32),
        ],
        scratch_shapes=[
            pltpu.VMEM((rows + more, WIDE), BF16),
            pltpu.VMEM((rows + more, 2 * half), F32),
            pltpu.VMEM((rows + more, 2 * half), F32),
            pltpu.VMEM((rows + more, 128), F32),
            pltpu.VMEM((CHUNK // 128, rows, 128), F32),
            pltpu.VMEM((rows, CHUNK), BF16),
        ],
        compiler_params=pltpu.CompilerParams(vmem_limit_bytes=VMEM),
        cost_estimate=pl.CostEstimate(
            flops=8 * (rows + more) * width * half, bytes_accessed=2 * rows * width + 8 * width * half, transcendentals=0
        ),
    )(received, received, received, wg0, wg1, wu0, wu1)


def down_kernel(blocks, slots, extra, chunks, hid, wd0, wd1, out, stack, wide):
    i = pl.program_id(0)
    rows, more = blocks * slots, blocks * extra
    parts = WIDE // CHUNK

    @pl.when(i < chunks)
    def _():
        both = jnp.concatenate([wd0[...], wd1[...]], axis=0)
        high = rows // DOWN_PIECES
        for at in range(0, rows, high):
            out[at : at + high, :] = jnp.dot(
                hid[at : at + high, :], both, preferred_element_type=F32
            ).astype(BF16)
        result = jnp.dot(hid[rows : rows + more, :], both, preferred_element_type=F32).astype(BF16)
        for part in range(parts):
            at = pl.multiple_of((i * parts + part) * more, more)
            stack[pl.ds(at, more), :] = result[:, part * CHUNK : (part + 1) * CHUNK]

    @pl.when(i == chunks)
    def _():
        to_blocks(wide, stack, out, blocks, slots)


def down(hid, wd0, wd1, blocks, slots, extra):
    half, width = wd0.shape
    chunks = width // WIDE
    rows = blocks * slots
    w_out = pl.BlockSpec((half, WIDE), lambda i: (0, jnp.minimum(i, chunks - 1)))
    return pl.pallas_call(
        functools.partial(down_kernel, blocks, slots, extra, chunks),
        grid=(chunks + 1,),
        in_specs=[pl.BlockSpec(hid.shape, lambda i: (0, 0)), w_out, w_out],
        out_specs=pl.BlockSpec((rows, WIDE), lambda i: (0, i)),
        out_shape=jax.ShapeDtypeStruct((rows, width + CHUNK), BF16),
        scratch_shapes=[pltpu.VMEM((rows, CHUNK), BF16), pltpu.VMEM((CHUNK // 128, rows, 128), F32)],
        compiler_params=pltpu.CompilerParams(vmem_limit_bytes=VMEM),
        cost_estimate=pl.CostEstimate(
            flops=4 * hid.shape[0] * width * half, bytes_accessed=2 * rows * width + 4 * width * half, transcendentals=0
        ),
    )(hid, wd0, wd1)


def after(value, *first):
    anywhere = pl.BlockSpec(memory_space=pl.ANY)
    return pl.pallas_call(
        lambda *refs: None,
        in_specs=[anywhere] * (1 + len(first)),
        out_specs=anywhere,
        out_shape=jax.ShapeDtypeStruct(value.shape, value.dtype),
        input_output_aliases={0: 0},
        cost_estimate=pl.CostEstimate(flops=0, bytes_accessed=0, transcendentals=0),
    )(value, *first)


def column(line):
    eye = iota((128, 128), 0) == iota((128, 128), 1)
    return jnp.concatenate(
        [
            jnp.sum(jnp.where(eye, line[:, at : at + 128], 0.0), axis=1, keepdims=True)
            for at in range(0, line.shape[1], 128)
        ],
        axis=0,
    )


def combine_kernel(experts, slots, extra, back, back_more, x, x_more, own, other, own_hid, other_hid, wg, wu, wd,
                   out, s_gate, s_up, s_down, wide, late):
    i = pl.program_id(0)
    more, parts = experts * extra, NARROW // CHUNK

    @pl.when(i == 0)
    def _():
        to_chunks(wide, x_more, late, experts, slots)

    total = jnp.dot(back[...], x[...], preferred_element_type=F32)
    for part in range(parts):
        lanes = slice(part * CHUNK, (part + 1) * CHUNK)
        at = pl.multiple_of((i * parts + part) * more, more)
        out[:, lanes] = (
            total[:, lanes] + jnp.dot(back_more[...], late[pl.ds(at, more), :], preferred_element_type=F32)
        ).astype(BF16)
    norm = column(jnp.sqrt(own[...] + other[...]))
    s_gate[...] = (jnp.abs(wg[...].astype(F32)) * norm).astype(BF16)
    s_up[...] = (jnp.abs(wu[...].astype(F32)) * norm).astype(BF16)
    half = wg.shape[1]
    norm = column(jnp.sqrt(own_hid[:, 0:half] + other_hid[:, half : 2 * half]))
    s_down[...] = (jnp.abs(wd[...].astype(F32)) * norm).astype(BF16)


def combine(back, back_more, returned, own, other, wg, wu, wd, experts, slots, extra):
    rows, wide = returned.shape
    width = wide - CHUNK
    chunks = width // NARROW
    count, half = back.shape[0], wg.shape[1]
    tall = pl.BlockSpec((NARROW, half), lambda i: (i, 0))
    flat = pl.BlockSpec((half, NARROW), lambda i: (0, i))
    sums = pl.BlockSpec((1, NARROW), lambda i: (0, i))
    last = pl.BlockSpec((1, WIDE), lambda i: (0, width // WIDE))
    return pl.pallas_call(
        functools.partial(combine_kernel, experts, slots, extra),
        grid=(chunks,),
        in_specs=[
            pl.BlockSpec(back.shape, lambda i: (0, 0)),
            pl.BlockSpec(back_more.shape, lambda i: (0, 0)),
            pl.BlockSpec((rows, NARROW), lambda i: (0, i)),
            pl.BlockSpec((rows, CHUNK), lambda i: (0, width // CHUNK)),
            sums, sums, last, last,
            tall, tall, flat,
        ],
        out_specs=[pl.BlockSpec((count, NARROW), lambda i: (0, i)), tall, tall, flat],
        out_shape=[
            jax.ShapeDtypeStruct((count, width), BF16),
            jax.ShapeDtypeStruct(wg.shape, BF16),
            jax.ShapeDtypeStruct(wu.shape, BF16),
            jax.ShapeDtypeStruct(wd.shape, BF16),
        ],
        scratch_shapes=[pltpu.VMEM((CHUNK // 128, rows, 128), F32), pltpu.VMEM((rows, CHUNK), BF16)],
        compiler_params=pltpu.CompilerParams(vmem_limit_bytes=VMEM),
        cost_estimate=pl.CostEstimate(flops=4 * rows * count * width, bytes_accessed=6 * rows * wide, transcendentals=0),
    )(back, back_more, returned, returned, own, other, own, other, wg, wu, wd)


def swap(value):
    return lax.ppermute(value, "tp", [(0, 1), (1, 0)])


def exchange(value, experts, slots):
    value = value.reshape(experts, slots, value.shape[1])
    value = lax.all_to_all(value, "exp", split_axis=0, concat_axis=0, tiled=True)
    return value.reshape(experts * slots, value.shape[2])


def per_device(tokens, gate_weight, up_weight, down_weight, routes, gate_probs, valid_mask):
    count, top = routes.shape
    experts = lax.axis_size("exp")
    cap = max(2, count * top * 9 // (8 * experts))
    extra = 2
    slots = cap - extra
    w_gate, w_up, w_down = gate_weight[0], up_weight[0], down_weight[0]
    o_gate, o_up = swap(w_gate), swap(w_up)
    routes, valid_mask, gate_probs = routes.T, valid_mask.T, gate_probs.T
    sent, back, back_more, late_down = build(
        routes, valid_mask, gate_probs, tokens, w_down, experts, slots, extra
    )
    received = exchange(after(sent, o_gate, o_up), experts, slots)
    o_down = swap(after(late_down, received))
    hid, sums = hidden_units(received, w_gate, o_gate, w_up, o_up, experts, slots, extra)
    other = swap(sums)
    outs = after(down(hid, w_down, o_down, experts, slots, extra), other)
    returned = exchange(outs, experts, slots)
    mixed, score_gate, score_up, score_down = combine(
        back, back_more, returned, sums, other, w_gate, w_up, w_down, experts, slots, extra
    )
    return (mixed, score_gate[None], score_up[None], score_down[None])


def solution(mesh):
    in_specs = (
        P(("exp", "tp"), None),
        P("exp", None, "tp"),
        P("exp", None, "tp"),
        P("exp", "tp", None),
        P(("exp", "tp"), None),
        P(("exp", "tp"), None),
        P(("exp", "tp"), None),
    )
    out_specs = (
        P(("exp", "tp"), None),
        P("exp", None, "tp"),
        P("exp", None, "tp"),
        P("exp", "tp", None),
    )
    return jax.shard_map(
        per_device, mesh=mesh, in_specs=in_specs, out_specs=out_specs, check_vma=False
    )
```

```python
import functools

import jax
import jax.numpy as jnp
from jax import lax
from jax.experimental import pallas as pl
from jax.experimental.pallas import tpu as pltpu
from jax.sharding import PartitionSpec as P

BF16, F32 = jnp.bfloat16, jnp.float32
CHUNK = 512
WIDE = 1024
PIECES = 8
DOWN_PIECES = 2
NARROW = 1024
VMEM = 56 * 1024 * 1024
COMBINE_VMEM = 28 * 1024 * 1024


def iota(shape, dim):
    return lax.broadcasted_iota(jnp.int32, shape, dim)


def one_hot(match):
    return jnp.where(match, 1.0, 0.0).astype(BF16)


def planes(width):
    return [(plane, slice(plane * 128, (plane + 1) * 128)) for plane in range(width // 128)]


def to_chunks(wide, packed, by_chunk, blocks, slots):
    for plane, lanes in planes(CHUNK):
        wide[plane] = packed[:, lanes].astype(F32)
        for at in range(slots):
            picked = wide[plane, pl.ds(at, blocks, stride=slots), :]
            by_chunk[at * blocks : (at + 1) * blocks, lanes] = picked.astype(BF16)


def to_blocks(wide, by_chunk, packed, blocks, slots):
    for plane, lanes in planes(CHUNK):
        for at in range(slots):
            rows = by_chunk[at * blocks : (at + 1) * blocks, lanes]
            wide[plane, pl.ds(at, blocks, stride=slots), :] = rows.astype(F32)
        packed[:, lanes] = wide[plane].astype(BF16)


def assign(experts, routes, valid, probs):
    count = routes.shape[1]
    ids = iota((experts, count), 0)
    named, weight = jnp.zeros((experts, count), F32), jnp.zeros((experts, count), F32)
    for k in range(routes.shape[0]):
        hit = (routes[k : k + 1, :] == ids) & (valid[k : k + 1, :] > 0)
        named = named + jnp.where(hit, 1.0, 0.0)
        weight = weight + jnp.where(hit, probs[k : k + 1, :], 0.0)
    before = one_hot(iota((count, count), 0) < iota((count, count), 1))
    place = jnp.dot(named.astype(BF16), before, preferred_element_type=F32)
    return jnp.where(named > 0, place, -1.0).astype(jnp.int32), weight


def build_kernel(experts, slots, extra, chunks, routes, valid, probs, tok, wd, out, back, back_more, wd_copy, sel_scr, pick_scr, stack, wide, w_scr):
    i = pl.program_id(0)
    more = experts * extra
    count = routes.shape[1]
    rows = experts * slots
    row = iota((experts, slots, count), 1)

    @pl.when(i == 0)
    def _():
        slot, weight = assign(experts, routes, valid, probs)
        slot, weight = slot.reshape(experts, 1, count), weight.reshape(experts, 1, count)
        hits = slot == row
        sel_scr[...] = jnp.where(hits, 1.0, 0.0).reshape(rows, count).astype(BF16)
        w_main = jnp.sum(jnp.where(hits, weight, 0.0), axis=2, keepdims=True)
        w_more = jnp.sum(jnp.where((slot == row + slots) & (row < extra), weight, 0.0), axis=2, keepdims=True)
        lane = iota((experts, slots, 128), 2)
        packed = jnp.where(lane == 0, w_main, jnp.where(lane == 1, w_more, 0.0))
        w_scr[...] = packed.reshape(rows, 128).astype(BF16)
        back[...] = jnp.where(hits, weight, 0.0).reshape(rows, count).T.astype(BF16)
        for r in range(extra):
            late = (slot == slots + r).reshape(experts, count)
            pick_scr[r * experts : (r + 1) * experts, :] = jnp.where(late, 1.0, 0.0).astype(BF16)
        late = [jnp.where(slot == slots + r, weight, 0.0).reshape(experts, count) for r in range(extra)]
        back_more[...] = jnp.concatenate(late, axis=0).T.astype(BF16)

    @pl.when(i < chunks)
    def _():
        wd_copy[...] = wd[...]
        out[...] = jnp.dot(sel_scr[...], tok[...], preferred_element_type=F32).astype(BF16)
        late = jnp.dot(pick_scr[...], tok[...], preferred_element_type=F32).astype(BF16)
        for part in range(WIDE // CHUNK):
            at = pl.multiple_of((i * (WIDE // CHUNK) + part) * more, more)
            stack[pl.ds(at, more), :] = late[:, part * CHUNK : (part + 1) * CHUNK]

    @pl.when(i == chunks)
    def _():
        to_blocks(wide, stack, out, experts, slots)
        out[:, CHUNK : CHUNK + 128] = w_scr[...]


def build(routes, valid, probs, tokens, wd, experts, slots, extra):
    count, width = tokens.shape
    chunks = width // WIDE
    rows = experts * slots
    small = pl.BlockSpec((routes.shape[0], count), lambda i: (0, 0))
    flat = pl.BlockSpec((wd.shape[0], WIDE), lambda i: (0, jnp.minimum(i, chunks - 1)))
    return pl.pallas_call(
        functools.partial(build_kernel, experts, slots, extra, chunks),
        grid=(chunks + 1,),
        in_specs=[small, small, small, pl.BlockSpec((count, WIDE), lambda i: (0, jnp.minimum(i, chunks - 1))), flat],
        out_specs=[
            pl.BlockSpec((rows, WIDE), lambda i: (0, i)),
            pl.BlockSpec((count, rows), lambda i: (0, 0)),
            pl.BlockSpec((count, experts * extra), lambda i: (0, 0)),
            flat,
        ],
        out_shape=[
            jax.ShapeDtypeStruct((rows, width + CHUNK + 128), BF16),
            jax.ShapeDtypeStruct((count, rows), BF16),
            jax.ShapeDtypeStruct((count, experts * extra), BF16),
            jax.ShapeDtypeStruct(wd.shape, BF16),
        ],
        scratch_shapes=[
            pltpu.VMEM((rows, count), BF16),
            pltpu.VMEM((experts * extra, count), BF16),
            pltpu.VMEM((rows, CHUNK), BF16),
            pltpu.VMEM((CHUNK // 128, rows, 128), F32),
            pltpu.VMEM((rows, 128), BF16),
        ],
        compiler_params=pltpu.CompilerParams(vmem_limit_bytes=VMEM),
        cost_estimate=pl.CostEstimate(flops=4 * rows * count * width, bytes_accessed=2 * rows * width, transcendentals=0),
    )(routes, valid, probs, tokens, wd)


def hidden_kernel(blocks, slots, extra, chunks, x, x_more, x_w, wg0, wg1, wu0, wu1, hid, sq, xs, acc0, acc1, w_col,
                  wide, late):
    i = pl.program_id(0)
    rows, more = blocks * slots, blocks * extra
    half = wg0.shape[1]
    parts = WIDE // CHUNK

    def fill():
        xs[0:rows, :] = x[...]
        for part in range(parts):
            at = pl.multiple_of((i * parts + part) * more, more)
            xs[rows : rows + more, part * CHUNK : (part + 1) * CHUNK] = late[pl.ds(at, more), :]

    def squares(lane):
        part = xs[:, lane : lane + 128].astype(F32)
        sq[:, lane : lane + 128] = jnp.sum(part * part * w_col[...], axis=0, keepdims=True)

    def products(use):
        high = (rows + more) // PIECES
        share = WIDE // PIECES
        for piece in range(PIECES):
            span = slice(piece * high, (piece + 1) * high)
            value = xs[span, :]
            for start, acc, gate, up in ((0, acc0, wg0, wu0), (half, acc1, wg1, wu1)):
                use(span, start, acc, jnp.dot(
                    value, jnp.concatenate([gate[...], up[...]], axis=1), preferred_element_type=F32
                ))
            for lane in range(piece * share, (piece + 1) * share, 128):
                squares(lane)

    def put(span, start, acc, product):
        acc[span, :] = product

    def add(span, start, acc, product):
        acc[span, :] += product

    def finish(span, start, acc, product):
        gate = acc[span, 0:half] + product[:, 0:half]
        up = acc[span, half : 2 * half] + product[:, half : 2 * half]
        hid[span, start : start + half] = (gate * (0.5 + 0.5 * jnp.tanh(0.5 * gate)) * up).astype(BF16)

    @pl.when(i == 0)
    def _():
        wide[0] = x_w[...].astype(F32)
        w_col[0:rows, :] = jnp.broadcast_to(wide[0, :, 0:1], (rows, 128))
        for r in range(extra):
            w_more = wide[0, pl.ds(r, blocks, stride=slots), :]
            w_col[rows + r * blocks : rows + (r + 1) * blocks, :] = jnp.broadcast_to(w_more[:, 1:2], (blocks, 128))
        to_chunks(wide, x_more, late, blocks, slots)
        fill()
        products(put)

    @pl.when((i > 0) & (i < chunks - 1))
    def _():
        fill()
        products(add)

    @pl.when(i == chunks - 1)
    def _():
        fill()
        products(finish)

    @pl.when(i == chunks)
    def _():
        sq[...] = jnp.zeros_like(sq)
        for lane in range(0, 2 * half, 128):
            value = hid[:, lane : lane + 128].astype(F32)
            sq[:, lane : lane + 128] = jnp.sum(value * value * w_col[...], axis=0, keepdims=True)


def hidden_units(received, wg0, wg1, wu0, wu1, blocks, slots, extra):
    width, half = wg0.shape
    chunks = width // WIDE
    rows, more = blocks * slots, blocks * extra
    up_to = lambda i: jnp.minimum(i, chunks - 1)
    w_in = pl.BlockSpec((WIDE, half), lambda i: (up_to(i), 0))
    return pl.pallas_call(
        functools.partial(hidden_kernel, blocks, slots, extra, chunks),
        grid=(chunks + 1,),
        in_specs=[
            pl.BlockSpec((rows, WIDE), lambda i: (0, up_to(i))),
            pl.BlockSpec((rows, CHUNK), lambda i: (0, width // CHUNK)),
            pl.BlockSpec((rows, 128), lambda i: (0, (width + CHUNK) // 128)),
            w_in, w_in, w_in, w_in,
        ],
        out_specs=[
            pl.BlockSpec((rows + more, 2 * half), lambda i: (0, 0)),
            pl.BlockSpec((1, WIDE), lambda i: (0, i)),
        ],
        out_shape=[
            jax.ShapeDtypeStruct((rows + more, 2 * half), BF16),
            jax.ShapeDtypeStruct((1, width + WIDE), F32),
        ],
        scratch_shapes=[
            pltpu.VMEM((rows + more, WIDE), BF16),
            pltpu.VMEM((rows + more, 2 * half), F32),
            pltpu.VMEM((rows + more, 2 * half), F32),
            pltpu.VMEM((rows + more, 128), F32),
            pltpu.VMEM((CHUNK // 128, rows, 128), F32),
            pltpu.VMEM((rows, CHUNK), BF16),
        ],
        compiler_params=pltpu.CompilerParams(vmem_limit_bytes=VMEM),
        cost_estimate=pl.CostEstimate(
            flops=8 * (rows + more) * width * half, bytes_accessed=2 * rows * width + 8 * width * half, transcendentals=0
        ),
    )(received, received, received, wg0, wg1, wu0, wu1)


def down_kernel(blocks, slots, extra, chunks, hid, wd0, wd1, out, stack, wide):
    i = pl.program_id(0)
    rows, more = blocks * slots, blocks * extra
    parts = WIDE // CHUNK

    @pl.when(i < chunks)
    def _():
        both = jnp.concatenate([wd0[...], wd1[...]], axis=0)
        high = rows // DOWN_PIECES
        for at in range(0, rows, high):
            out[at : at + high, :] = jnp.dot(
                hid[at : at + high, :], both, preferred_element_type=F32
            ).astype(BF16)
        result = jnp.dot(hid[rows : rows + more, :], both, preferred_element_type=F32).astype(BF16)
        for part in range(parts):
            at = pl.multiple_of((i * parts + part) * more, more)
            stack[pl.ds(at, more), :] = result[:, part * CHUNK : (part + 1) * CHUNK]

    @pl.when(i == chunks)
    def _():
        to_blocks(wide, stack, out, blocks, slots)


def down(hid, wd0, wd1, blocks, slots, extra):
    half, width = wd0.shape
    chunks = width // WIDE
    rows = blocks * slots
    w_out = pl.BlockSpec((half, WIDE), lambda i: (0, jnp.minimum(i, chunks - 1)))
    return pl.pallas_call(
        functools.partial(down_kernel, blocks, slots, extra, chunks),
        grid=(chunks + 1,),
        in_specs=[pl.BlockSpec(hid.shape, lambda i: (0, 0)), w_out, w_out],
        out_specs=pl.BlockSpec((rows, WIDE), lambda i: (0, i)),
        out_shape=jax.ShapeDtypeStruct((rows, width + CHUNK), BF16),
        scratch_shapes=[pltpu.VMEM((rows, CHUNK), BF16), pltpu.VMEM((CHUNK // 128, rows, 128), F32)],
        compiler_params=pltpu.CompilerParams(vmem_limit_bytes=VMEM),
        cost_estimate=pl.CostEstimate(
            flops=4 * hid.shape[0] * width * half, bytes_accessed=2 * rows * width + 4 * width * half, transcendentals=0
        ),
    )(hid, wd0, wd1)


def after(value, *first):
    anywhere = pl.BlockSpec(memory_space=pl.ANY)
    return pl.pallas_call(
        lambda *refs: None,
        in_specs=[anywhere] * (1 + len(first)),
        out_specs=anywhere,
        out_shape=jax.ShapeDtypeStruct(value.shape, value.dtype),
        input_output_aliases={0: 0},
        cost_estimate=pl.CostEstimate(flops=0, bytes_accessed=0, transcendentals=0),
    )(value, *first)


def column(line):
    eye = iota((128, 128), 0) == iota((128, 128), 1)
    return jnp.concatenate(
        [
            jnp.sum(jnp.where(eye, line[:, at : at + 128], 0.0), axis=1, keepdims=True)
            for at in range(0, line.shape[1], 128)
        ],
        axis=0,
    )


def combine_kernel(experts, slots, extra, back, back_more, x, x_more, own, other, own_hid, other_hid, wg, wu, wd,
                   out, s_gate, s_up, s_down, wide, late):
    i = pl.program_id(0)
    more, parts = experts * extra, NARROW // CHUNK

    @pl.when(i == 0)
    def _():
        to_chunks(wide, x_more, late, experts, slots)

    total = jnp.dot(back[...], x[...], preferred_element_type=F32)
    for part in range(parts):
        lanes = slice(part * CHUNK, (part + 1) * CHUNK)
        at = pl.multiple_of((i * parts + part) * more, more)
        out[:, lanes] = (
            total[:, lanes] + jnp.dot(back_more[...], late[pl.ds(at, more), :], preferred_element_type=F32)
        ).astype(BF16)
    norm = column(jnp.sqrt(own[...] + other[...]))
    s_gate[...] = (jnp.abs(wg[...].astype(F32)) * norm).astype(BF16)
    s_up[...] = (jnp.abs(wu[...].astype(F32)) * norm).astype(BF16)
    half = wg.shape[1]
    norm = column(jnp.sqrt(own_hid[:, 0:half] + other_hid[:, half : 2 * half]))
    s_down[...] = (jnp.abs(wd[...].astype(F32)) * norm).astype(BF16)


def combine(back, back_more, returned, own, other, wg, wu, wd, experts, slots, extra):
    rows, wide = returned.shape
    width = wide - CHUNK
    chunks = width // NARROW
    count, half = back.shape[0], wg.shape[1]
    tall = pl.BlockSpec((NARROW, half), lambda i: (i, 0))
    flat = pl.BlockSpec((half, NARROW), lambda i: (0, i))
    sums = pl.BlockSpec((1, NARROW), lambda i: (0, i))
    last = pl.BlockSpec((1, WIDE), lambda i: (0, width // WIDE))
    return pl.pallas_call(
        functools.partial(combine_kernel, experts, slots, extra),
        grid=(chunks,),
        in_specs=[
            pl.BlockSpec(back.shape, lambda i: (0, 0)),
            pl.BlockSpec(back_more.shape, lambda i: (0, 0)),
            pl.BlockSpec((rows, NARROW), lambda i: (0, i)),
            pl.BlockSpec((rows, CHUNK), lambda i: (0, width // CHUNK)),
            sums, sums, last, last,
            tall, tall, flat,
        ],
        out_specs=[pl.BlockSpec((count, NARROW), lambda i: (0, i)), tall, tall, flat],
        out_shape=[
            jax.ShapeDtypeStruct((count, width), BF16),
            jax.ShapeDtypeStruct(wg.shape, BF16),
            jax.ShapeDtypeStruct(wu.shape, BF16),
            jax.ShapeDtypeStruct(wd.shape, BF16),
        ],
        scratch_shapes=[pltpu.VMEM((CHUNK // 128, rows, 128), F32), pltpu.VMEM((rows, CHUNK), BF16)],
        compiler_params=pltpu.CompilerParams(vmem_limit_bytes=COMBINE_VMEM),
        cost_estimate=pl.CostEstimate(flops=4 * rows * count * width, bytes_accessed=6 * rows * wide, transcendentals=0),
    )(back, back_more, returned, returned, own, other, own, other, wg, wu, wd)


def swap(value):
    return lax.ppermute(value, "tp", [(0, 1), (1, 0)])


def exchange(value, experts, slots):
    value = value.reshape(experts, slots, value.shape[1])
    value = lax.all_to_all(value, "exp", split_axis=0, concat_axis=0, tiled=True)
    return value.reshape(experts * slots, value.shape[2])


def per_device(tokens, gate_weight, up_weight, down_weight, routes, gate_probs, valid_mask):
    count, top = routes.shape
    experts = lax.axis_size("exp")
    cap = max(2, count * top * 9 // (8 * experts))
    extra = 2
    slots = cap - extra
    w_gate, w_up, w_down = gate_weight[0], up_weight[0], down_weight[0]
    o_gate, o_up = swap(w_gate), swap(w_up)
    routes, valid_mask, gate_probs = routes.T, valid_mask.T, gate_probs.T
    sent, back, back_more, late_down = build(
        routes, valid_mask, gate_probs, tokens, w_down, experts, slots, extra
    )
    received = exchange(after(sent, o_gate, o_up), experts, slots)
    o_down = swap(after(late_down, received))
    hid, sums = hidden_units(received, w_gate, o_gate, w_up, o_up, experts, slots, extra)
    other = swap(sums)
    outs = after(down(hid, w_down, o_down, experts, slots, extra), other)
    returned = exchange(outs, experts, slots)
    mixed, score_gate, score_up, score_down = combine(
        back, back_more, returned, sums, other, w_gate, w_up, w_down, experts, slots, extra
    )
    return (mixed, score_gate[None], score_up[None], score_down[None])


def solution(mesh):
    in_specs = (
        P(("exp", "tp"), None),
        P("exp", None, "tp"),
        P("exp", None, "tp"),
        P("exp", "tp", None),
        P(("exp", "tp"), None),
        P(("exp", "tp"), None),
        P(("exp", "tp"), None),
    )
    out_specs = (
        P(("exp", "tp"), None),
        P("exp", None, "tp"),
        P("exp", None, "tp"),
        P("exp", "tp", None),
    )
    return jax.shard_map(
        per_device, mesh=mesh, in_specs=in_specs, out_specs=out_specs, check_vma=False
    )
```

```python
import functools

import jax
import jax.numpy as jnp
from jax import lax
from jax.experimental import pallas as pl
from jax.experimental.pallas import tpu as pltpu
from jax.sharding import PartitionSpec as P

BF16, F32 = jnp.bfloat16, jnp.float32
CHUNK = 512
WIDE = 1024
PIECES = 8
DOWN_PIECES = 2
NARROW = 1024
VMEM = 56 * 1024 * 1024
COMBINE_VMEM = 28 * 1024 * 1024
DOWN_VMEM = 22 * 1024 * 1024


def iota(shape, dim):
    return lax.broadcasted_iota(jnp.int32, shape, dim)


def one_hot(match):
    return jnp.where(match, 1.0, 0.0).astype(BF16)


def planes(width):
    return [(plane, slice(plane * 128, (plane + 1) * 128)) for plane in range(width // 128)]


def to_chunks(wide, packed, by_chunk, blocks, slots):
    for plane, lanes in planes(CHUNK):
        wide[plane] = packed[:, lanes].astype(F32)
        for at in range(slots):
            picked = wide[plane, pl.ds(at, blocks, stride=slots), :]
            by_chunk[at * blocks : (at + 1) * blocks, lanes] = picked.astype(BF16)


def to_blocks(wide, by_chunk, packed, blocks, slots):
    for plane, lanes in planes(CHUNK):
        for at in range(slots):
            rows = by_chunk[at * blocks : (at + 1) * blocks, lanes]
            wide[plane, pl.ds(at, blocks, stride=slots), :] = rows.astype(F32)
        packed[:, lanes] = wide[plane].astype(BF16)


def assign(experts, routes, valid, probs):
    count = routes.shape[1]
    ids = iota((experts, count), 0)
    named, weight = jnp.zeros((experts, count), F32), jnp.zeros((experts, count), F32)
    for k in range(routes.shape[0]):
        hit = (routes[k : k + 1, :] == ids) & (valid[k : k + 1, :] > 0)
        named = named + jnp.where(hit, 1.0, 0.0)
        weight = weight + jnp.where(hit, probs[k : k + 1, :], 0.0)
    before = one_hot(iota((count, count), 0) < iota((count, count), 1))
    place = jnp.dot(named.astype(BF16), before, preferred_element_type=F32)
    return jnp.where(named > 0, place, -1.0).astype(jnp.int32), weight


def build_kernel(experts, slots, extra, chunks, routes, valid, probs, tok, wd, out, back, back_more, wd_copy, sel_scr, pick_scr, stack, wide, w_scr):
    i = pl.program_id(0)
    more = experts * extra
    count = routes.shape[1]
    rows = experts * slots
    row = iota((experts, slots, count), 1)

    @pl.when(i == 0)
    def _():
        slot, weight = assign(experts, routes, valid, probs)
        slot, weight = slot.reshape(experts, 1, count), weight.reshape(experts, 1, count)
        hits = slot == row
        sel_scr[...] = jnp.where(hits, 1.0, 0.0).reshape(rows, count).astype(BF16)
        w_main = jnp.sum(jnp.where(hits, weight, 0.0), axis=2, keepdims=True)
        w_more = jnp.sum(jnp.where((slot == row + slots) & (row < extra), weight, 0.0), axis=2, keepdims=True)
        lane = iota((experts, slots, 128), 2)
        packed = jnp.where(lane == 0, w_main, jnp.where(lane == 1, w_more, 0.0))
        w_scr[...] = packed.reshape(rows, 128).astype(BF16)
        back[...] = jnp.where(hits, weight, 0.0).reshape(rows, count).T.astype(BF16)
        for r in range(extra):
            late = (slot == slots + r).reshape(experts, count)
            pick_scr[r * experts : (r + 1) * experts, :] = jnp.where(late, 1.0, 0.0).astype(BF16)
        late = [jnp.where(slot == slots + r, weight, 0.0).reshape(experts, count) for r in range(extra)]
        back_more[...] = jnp.concatenate(late, axis=0).T.astype(BF16)

    @pl.when(i < chunks)
    def _():
        wd_copy[...] = wd[...]
        out[...] = jnp.dot(sel_scr[...], tok[...], preferred_element_type=F32).astype(BF16)
        late = jnp.dot(pick_scr[...], tok[...], preferred_element_type=F32).astype(BF16)
        for part in range(WIDE // CHUNK):
            at = pl.multiple_of((i * (WIDE // CHUNK) + part) * more, more)
            stack[pl.ds(at, more), :] = late[:, part * CHUNK : (part + 1) * CHUNK]

    @pl.when(i == chunks)
    def _():
        to_blocks(wide, stack, out, experts, slots)
        out[:, CHUNK : CHUNK + 128] = w_scr[...]


def build(routes, valid, probs, tokens, wd, experts, slots, extra):
    count, width = tokens.shape
    chunks = width // WIDE
    rows = experts * slots
    small = pl.BlockSpec((routes.shape[0], count), lambda i: (0, 0))
    flat = pl.BlockSpec((wd.shape[0], WIDE), lambda i: (0, jnp.minimum(i, chunks - 1)))
    return pl.pallas_call(
        functools.partial(build_kernel, experts, slots, extra, chunks),
        grid=(chunks + 1,),
        in_specs=[small, small, small, pl.BlockSpec((count, WIDE), lambda i: (0, jnp.minimum(i, chunks - 1))), flat],
        out_specs=[
            pl.BlockSpec((rows, WIDE), lambda i: (0, i)),
            pl.BlockSpec((count, rows), lambda i: (0, 0)),
            pl.BlockSpec((count, experts * extra), lambda i: (0, 0)),
            flat,
        ],
        out_shape=[
            jax.ShapeDtypeStruct((rows, width + CHUNK + 128), BF16),
            jax.ShapeDtypeStruct((count, rows), BF16),
            jax.ShapeDtypeStruct((count, experts * extra), BF16),
            jax.ShapeDtypeStruct(wd.shape, BF16),
        ],
        scratch_shapes=[
            pltpu.VMEM((rows, count), BF16),
            pltpu.VMEM((experts * extra, count), BF16),
            pltpu.VMEM((rows, CHUNK), BF16),
            pltpu.VMEM((CHUNK // 128, rows, 128), F32),
            pltpu.VMEM((rows, 128), BF16),
        ],
        compiler_params=pltpu.CompilerParams(vmem_limit_bytes=VMEM),
        cost_estimate=pl.CostEstimate(flops=4 * rows * count * width, bytes_accessed=2 * rows * width, transcendentals=0),
    )(routes, valid, probs, tokens, wd)


def hidden_kernel(blocks, slots, extra, chunks, x, x_more, x_w, wg0, wg1, wu0, wu1, hid, sq, xs, acc0, acc1, w_col,
                  wide, late):
    i = pl.program_id(0)
    rows, more = blocks * slots, blocks * extra
    half = wg0.shape[1]
    parts = WIDE // CHUNK

    def fill():
        xs[0:rows, :] = x[...]
        for part in range(parts):
            at = pl.multiple_of((i * parts + part) * more, more)
            xs[rows : rows + more, part * CHUNK : (part + 1) * CHUNK] = late[pl.ds(at, more), :]

    def squares(lane):
        part = xs[:, lane : lane + 128].astype(F32)
        sq[:, lane : lane + 128] = jnp.sum(part * part * w_col[...], axis=0, keepdims=True)

    def products(use):
        high = (rows + more) // PIECES
        share = WIDE // PIECES
        for piece in range(PIECES):
            span = slice(piece * high, (piece + 1) * high)
            value = xs[span, :]
            for start, acc, gate, up in ((0, acc0, wg0, wu0), (half, acc1, wg1, wu1)):
                use(span, start, acc, jnp.dot(
                    value, jnp.concatenate([gate[...], up[...]], axis=1), preferred_element_type=F32
                ))
            for lane in range(piece * share, (piece + 1) * share, 128):
                squares(lane)

    def put(span, start, acc, product):
        acc[span, :] = product

    def add(span, start, acc, product):
        acc[span, :] += product

    def finish(span, start, acc, product):
        gate = acc[span, 0:half] + product[:, 0:half]
        up = acc[span, half : 2 * half] + product[:, half : 2 * half]
        hid[span, start : start + half] = (gate * (0.5 + 0.5 * jnp.tanh(0.5 * gate)) * up).astype(BF16)

    @pl.when(i == 0)
    def _():
        wide[0] = x_w[...].astype(F32)
        w_col[0:rows, :] = jnp.broadcast_to(wide[0, :, 0:1], (rows, 128))
        for r in range(extra):
            w_more = wide[0, pl.ds(r, blocks, stride=slots), :]
            w_col[rows + r * blocks : rows + (r + 1) * blocks, :] = jnp.broadcast_to(w_more[:, 1:2], (blocks, 128))
        to_chunks(wide, x_more, late, blocks, slots)
        fill()
        products(put)

    @pl.when((i > 0) & (i < chunks - 1))
    def _():
        fill()
        products(add)

    @pl.when(i == chunks - 1)
    def _():
        fill()
        products(finish)

    @pl.when(i == chunks)
    def _():
        sq[...] = jnp.zeros_like(sq)
        for lane in range(0, 2 * half, 128):
            value = hid[:, lane : lane + 128].astype(F32)
            sq[:, lane : lane + 128] = jnp.sum(value * value * w_col[...], axis=0, keepdims=True)


def hidden_units(received, wg0, wg1, wu0, wu1, blocks, slots, extra):
    width, half = wg0.shape
    chunks = width // WIDE
    rows, more = blocks * slots, blocks * extra
    up_to = lambda i: jnp.minimum(i, chunks - 1)
    w_in = pl.BlockSpec((WIDE, half), lambda i: (up_to(i), 0))
    return pl.pallas_call(
        functools.partial(hidden_kernel, blocks, slots, extra, chunks),
        grid=(chunks + 1,),
        in_specs=[
            pl.BlockSpec((rows, WIDE), lambda i: (0, up_to(i))),
            pl.BlockSpec((rows, CHUNK), lambda i: (0, width // CHUNK)),
            pl.BlockSpec((rows, 128), lambda i: (0, (width + CHUNK) // 128)),
            w_in, w_in, w_in, w_in,
        ],
        out_specs=[
            pl.BlockSpec((rows + more, 2 * half), lambda i: (0, 0)),
            pl.BlockSpec((1, WIDE), lambda i: (0, i)),
        ],
        out_shape=[
            jax.ShapeDtypeStruct((rows + more, 2 * half), BF16),
            jax.ShapeDtypeStruct((1, width + WIDE), F32),
        ],
        scratch_shapes=[
            pltpu.VMEM((rows + more, WIDE), BF16),
            pltpu.VMEM((rows + more, 2 * half), F32),
            pltpu.VMEM((rows + more, 2 * half), F32),
            pltpu.VMEM((rows + more, 128), F32),
            pltpu.VMEM((CHUNK // 128, rows, 128), F32),
            pltpu.VMEM((rows, CHUNK), BF16),
        ],
        compiler_params=pltpu.CompilerParams(vmem_limit_bytes=VMEM),
        cost_estimate=pl.CostEstimate(
            flops=8 * (rows + more) * width * half, bytes_accessed=2 * rows * width + 8 * width * half, transcendentals=0
        ),
    )(received, received, received, wg0, wg1, wu0, wu1)


def down_kernel(blocks, slots, extra, chunks, hid, wd0, wd1, out, stack, wide):
    i = pl.program_id(0)
    rows, more = blocks * slots, blocks * extra
    parts = WIDE // CHUNK

    @pl.when(i < chunks)
    def _():
        both = jnp.concatenate([wd0[...], wd1[...]], axis=0)
        high = rows // DOWN_PIECES
        for at in range(0, rows, high):
            out[at : at + high, :] = jnp.dot(
                hid[at : at + high, :], both, preferred_element_type=F32
            ).astype(BF16)
        result = jnp.dot(hid[rows : rows + more, :], both, preferred_element_type=F32).astype(BF16)
        for part in range(parts):
            at = pl.multiple_of((i * parts + part) * more, more)
            stack[pl.ds(at, more), :] = result[:, part * CHUNK : (part + 1) * CHUNK]

    @pl.when(i == chunks)
    def _():
        to_blocks(wide, stack, out, blocks, slots)


def down(hid, wd0, wd1, blocks, slots, extra):
    half, width = wd0.shape
    chunks = width // WIDE
    rows = blocks * slots
    w_out = pl.BlockSpec((half, WIDE), lambda i: (0, jnp.minimum(i, chunks - 1)))
    return pl.pallas_call(
        functools.partial(down_kernel, blocks, slots, extra, chunks),
        grid=(chunks + 1,),
        in_specs=[pl.BlockSpec(hid.shape, lambda i: (0, 0)), w_out, w_out],
        out_specs=pl.BlockSpec((rows, WIDE), lambda i: (0, i)),
        out_shape=jax.ShapeDtypeStruct((rows, width + CHUNK), BF16),
        scratch_shapes=[pltpu.VMEM((rows, CHUNK), BF16), pltpu.VMEM((CHUNK // 128, rows, 128), F32)],
        compiler_params=pltpu.CompilerParams(vmem_limit_bytes=DOWN_VMEM),
        cost_estimate=pl.CostEstimate(
            flops=4 * hid.shape[0] * width * half, bytes_accessed=2 * rows * width + 4 * width * half, transcendentals=0
        ),
    )(hid, wd0, wd1)


def after(value, *first):
    anywhere = pl.BlockSpec(memory_space=pl.ANY)
    return pl.pallas_call(
        lambda *refs: None,
        in_specs=[anywhere] * (1 + len(first)),
        out_specs=anywhere,
        out_shape=jax.ShapeDtypeStruct(value.shape, value.dtype),
        input_output_aliases={0: 0},
        compiler_params=pltpu.CompilerParams(vmem_limit_bytes=VMEM),
        cost_estimate=pl.CostEstimate(flops=0, bytes_accessed=0, transcendentals=0),
    )(value, *first)


def column(line):
    eye = iota((128, 128), 0) == iota((128, 128), 1)
    return jnp.concatenate(
        [
            jnp.sum(jnp.where(eye, line[:, at : at + 128], 0.0), axis=1, keepdims=True)
            for at in range(0, line.shape[1], 128)
        ],
        axis=0,
    )


def combine_kernel(experts, slots, extra, back, back_more, x, x_more, own, other, own_hid, other_hid, wg, wu, wd,
                   out, s_gate, s_up, s_down, wide, late):
    i = pl.program_id(0)
    more, parts = experts * extra, NARROW // CHUNK

    @pl.when(i == 0)
    def _():
        to_chunks(wide, x_more, late, experts, slots)

    total = jnp.dot(back[...], x[...], preferred_element_type=F32)
    for part in range(parts):
        lanes = slice(part * CHUNK, (part + 1) * CHUNK)
        at = pl.multiple_of((i * parts + part) * more, more)
        out[:, lanes] = (
            total[:, lanes] + jnp.dot(back_more[...], late[pl.ds(at, more), :], preferred_element_type=F32)
        ).astype(BF16)
    norm = column(jnp.sqrt(own[...] + other[...]))
    s_gate[...] = (jnp.abs(wg[...].astype(F32)) * norm).astype(BF16)
    s_up[...] = (jnp.abs(wu[...].astype(F32)) * norm).astype(BF16)
    half = wg.shape[1]
    norm = column(jnp.sqrt(own_hid[:, 0:half] + other_hid[:, half : 2 * half]))
    s_down[...] = (jnp.abs(wd[...].astype(F32)) * norm).astype(BF16)


def combine(back, back_more, returned, own, other, wg, wu, wd, experts, slots, extra):
    rows, wide = returned.shape
    width = wide - CHUNK
    chunks = width // NARROW
    count, half = back.shape[0], wg.shape[1]
    tall = pl.BlockSpec((NARROW, half), lambda i: (i, 0))
    flat = pl.BlockSpec((half, NARROW), lambda i: (0, i))
    sums = pl.BlockSpec((1, NARROW), lambda i: (0, i))
    last = pl.BlockSpec((1, WIDE), lambda i: (0, width // WIDE))
    return pl.pallas_call(
        functools.partial(combine_kernel, experts, slots, extra),
        grid=(chunks,),
        in_specs=[
            pl.BlockSpec(back.shape, lambda i: (0, 0)),
            pl.BlockSpec(back_more.shape, lambda i: (0, 0)),
            pl.BlockSpec((rows, NARROW), lambda i: (0, i)),
            pl.BlockSpec((rows, CHUNK), lambda i: (0, width // CHUNK)),
            sums, sums, last, last,
            tall, tall, flat,
        ],
        out_specs=[pl.BlockSpec((count, NARROW), lambda i: (0, i)), tall, tall, flat],
        out_shape=[
            jax.ShapeDtypeStruct((count, width), BF16),
            jax.ShapeDtypeStruct(wg.shape, BF16),
            jax.ShapeDtypeStruct(wu.shape, BF16),
            jax.ShapeDtypeStruct(wd.shape, BF16),
        ],
        scratch_shapes=[pltpu.VMEM((CHUNK // 128, rows, 128), F32), pltpu.VMEM((rows, CHUNK), BF16)],
        compiler_params=pltpu.CompilerParams(vmem_limit_bytes=COMBINE_VMEM),
        cost_estimate=pl.CostEstimate(flops=4 * rows * count * width, bytes_accessed=6 * rows * wide, transcendentals=0),
    )(back, back_more, returned, returned, own, other, own, other, wg, wu, wd)


def swap(value):
    return lax.ppermute(value, "tp", [(0, 1), (1, 0)])


def exchange(value, experts, slots):
    value = value.reshape(experts, slots, value.shape[1])
    value = lax.all_to_all(value, "exp", split_axis=0, concat_axis=0, tiled=True)
    return value.reshape(experts * slots, value.shape[2])


def per_device(tokens, gate_weight, up_weight, down_weight, routes, gate_probs, valid_mask):
    count, top = routes.shape
    experts = lax.axis_size("exp")
    cap = max(2, count * top * 9 // (8 * experts))
    extra = 2
    slots = cap - extra
    w_gate, w_up, w_down = gate_weight[0], up_weight[0], down_weight[0]
    o_gate, o_up = swap(w_gate), swap(w_up)
    routes, valid_mask, gate_probs = routes.T, valid_mask.T, gate_probs.T
    sent, back, back_more, late_down = build(
        routes, valid_mask, gate_probs, tokens, w_down, experts, slots, extra
    )
    received = exchange(after(sent, o_gate, o_up), experts, slots)
    o_down = swap(after(late_down, received))
    hid, sums = hidden_units(received, w_gate, o_gate, w_up, o_up, experts, slots, extra)
    other = swap(sums)
    outs = after(down(hid, w_down, o_down, experts, slots, extra), other)
    returned = exchange(outs, experts, slots)
    mixed, score_gate, score_up, score_down = combine(
        back, back_more, returned, sums, other, w_gate, w_up, w_down, experts, slots, extra
    )
    return (mixed, score_gate[None], score_up[None], score_down[None])


def solution(mesh):
    in_specs = (
        P(("exp", "tp"), None),
        P("exp", None, "tp"),
        P("exp", None, "tp"),
        P("exp", "tp", None),
        P(("exp", "tp"), None),
        P(("exp", "tp"), None),
        P(("exp", "tp"), None),
    )
    out_specs = (
        P(("exp", "tp"), None),
        P("exp", None, "tp"),
        P("exp", None, "tp"),
        P("exp", "tp", None),
    )
    return jax.shard_map(
        per_device, mesh=mesh, in_specs=in_specs, out_specs=out_specs, check_vma=False
    )
```
